1024 devices in a mesh: dp: 32 (over z_hi, y, core), mp: 32 (over x, z_lo).
Axes of the slice: x: 4, y: 4, z: 32 (z_hi: 4, z_lo: 8; z = z_hi * 8 + z_lo), core: 2. Of those that a mesh axis runs over, the one named last changes fastest.
Arguments:
- layer_input: bfloat16 [6144, 3072], P(('dp', 'mp')), may hold values from -24 to 24
- out_grad: bfloat16 [6144, 3072], P(('dp', 'mp')), may hold values from -24 to 24
- norm_gain_vector: float32 [3072], replicated, may hold values from 0.5 to 1.5
- up_weight: bfloat16 [3072, 12288], P(None, 'mp'), may hold values from -0.109375 to 0.109375
- down_weight: bfloat16 [12288, 3072], P('mp'), may hold values from -0.0546875 to 0.0546875
Outputs:
- input_grad: bfloat16 [6144, 3072], P(('dp', 'mp'))
- up_grad: float32 [3072, 12288], P('dp', 'mp')
- down_grad: float32 [12288, 3072], P('mp', 'dp')
The draws below stay inside these ranges and needn't reach their ends.
All inputs are finite; a program needn't handle non-finite values.
Results may differ from the reference program's by a relative error of at most 0.02.
Values may be sent and summed in bfloat16 or wider, within the bound.
No kernel may reach another device: no remote copies, remote signals or barrier semaphores. Data moves between devices by JAX's collectives and lax.ppermute only.
A program may use at most 32 MiB of HBM per device.

```python
import math
import jax
import jax.numpy as jnp
from jax import lax

D = 3072
FF = 12288
TOK_GRP = 192
TOKENS = 6144
N_DP = 32
N_MP = 32


def raised(drawn, rng, source, target, blocks, factor):
    def block_of(dim):
        return (jnp.arange(drawn.shape[dim]) // (drawn.shape[dim] // blocks)).reshape((-1,) + (1,) * (drawn.ndim - 1 - dim))

    near = jax.random.permutation(rng, blocks)[block_of(target)]
    far = (block_of(target) + blocks // 2) % blocks
    return jnp.where((block_of(source) == near) | (block_of(source) == far), factor * drawn, drawn)


def levels(stream_key, shape, cuts, low, largest):
    factor_of, own = 1.0, jax.random.fold_in(stream_key, 6)
    for position, shards_of in cuts:
        steps = jnp.exp(jax.random.uniform(jax.random.fold_in(own, position), (shards_of,), jnp.float32, low / len(cuts), largest / len(cuts)))
        factor_of = factor_of * jnp.repeat(steps, shape[position] // shards_of).reshape([-1 if axis == position else 1 for axis in range(len(shape))])
    return factor_of


def normal_values(key, extent, scale, reach, split=(), held_as=jnp.bfloat16):
    gain = levels(key, extent, split, -0.22, 0.18) if split else 1.0
    array = jax.random.normal(key, extent, jnp.float32) * scale * gain
    return jnp.minimum(jnp.maximum(array, -reach), reach).astype(held_as)


def heavy_noise(own_key, shape, scale, bound, pieces, heavy, kind=jnp.bfloat16):
    values = scale * jax.random.normal(own_key, shape, jnp.float32)
    if pieces:
        values = values * levels(own_key, shape, pieces, -0.22, 0.18)
    return jnp.clip(raised(values, jax.random.fold_in(own_key, 3), *heavy), -bound, bound).astype(kind)


def setup_inputs(seed: int = 0) -> dict:
    arg_keys = jax.random.split(jax.random.key(seed), 6)
    layer_input = heavy_noise(arg_keys[0], (TOKENS, D), 1.0, 24.0, ((0, 1024),), (0, 1, 1024, 6.0))
    out_grad = heavy_noise(arg_keys[1], (TOKENS, D), 1.0, 24.0, ((0, 1024),), (0, 1, 1024, 6.0))
    norm_gain_vector = jnp.clip(1.0 + 0.1 * jax.random.normal(arg_keys[2], (D,), jnp.float32), 0.5, 1.5)
    up_weight = normal_values(arg_keys[3], (D, FF), D ** -0.5, 0.109375, ((1, 32),))
    down_weight = normal_values(arg_keys[4], (FF, D), FF ** -0.5, 0.0546875, ((0, 32),))
    return dict(layer_input=layer_input, out_grad=out_grad, norm_gain_vector=norm_gain_vector, up_weight=up_weight, down_weight=down_weight)


def gelu_value(v):
    return 0.5 * v * (1.0 + jax.scipy.special.erf(v / math.sqrt(2.0)))

def gelu_slope(v):
    return 0.5 * (1.0 + jax.scipy.special.erf(v / math.sqrt(2.0))) + v * jnp.exp(-0.5 * v * v) / math.sqrt(2.0 * math.pi)

def reference(layer_input, out_grad, norm_gain_vector, up_weight, down_weight):
    inputs = layer_input.reshape(N_DP, TOK_GRP, D)
    grads = out_grad.reshape(N_DP, TOK_GRP, D)
    width = FF // N_MP
    up_blocks = up_weight.astype(jnp.float32).reshape(D, N_MP, width)

    def one_group(carry, pair):
        up_total, down_total = carry
        xrow, dyrow = pair
        xf = xrow.astype(jnp.float32)
        mean_val = lax.optimization_barrier(jnp.mean(xf, axis=1, keepdims=True))
        centered_input = xf - mean_val
        inverse_deviation = 1.0 / jnp.sqrt(lax.optimization_barrier(jnp.mean(centered_input * centered_input, axis=1, keepdims=True)) + 1e-06)
        standardized_input = centered_input * inverse_deviation
        normalized_input = (standardized_input * norm_gain_vector).astype(jnp.bfloat16)
        pre = jnp.dot(normalized_input, up_weight, preferred_element_type=jnp.float32)
        hidden = gelu_value(pre).astype(jnp.bfloat16)
        hidden_grad = jnp.dot(dyrow, down_weight.T, preferred_element_type=jnp.float32)
        pre_grad = (hidden_grad * gelu_slope(pre)).astype(jnp.bfloat16)
        down_part = jnp.dot(hidden.T, dyrow, preferred_element_type=jnp.float32).astype(jnp.bfloat16)
        up_part = jnp.dot(normalized_input.T, pre_grad, preferred_element_type=jnp.float32).astype(jnp.bfloat16)
        grad_blocks = pre_grad.astype(jnp.float32).reshape(TOK_GRP, N_MP, width)
        partial_value = jnp.einsum('tkf,dkf->ktd', grad_blocks, up_blocks).astype(jnp.bfloat16)
        normed_grad = lax.optimization_barrier(jnp.sum(partial_value.astype(jnp.float32), axis=0))
        scaled_input = normed_grad * norm_gain_vector
        backward_pass = inverse_deviation * (scaled_input - lax.optimization_barrier(jnp.mean(scaled_input, axis=1, keepdims=True)) - standardized_input * lax.optimization_barrier(jnp.mean(scaled_input * standardized_input, axis=1, keepdims=True)))
        result = (dyrow.astype(jnp.float32) + backward_pass).astype(jnp.bfloat16)
        return ((up_total + up_part.astype(jnp.float32), down_total + down_part.astype(jnp.float32)), result)
    start = (jnp.zeros((D, FF), jnp.float32), jnp.zeros((FF, D), jnp.float32))
    (up_grad, down_grad), rows = lax.scan(one_group, start, (inputs, grads))
    return (rows.reshape(TOKENS, D), up_grad, down_grad)
```

```python
import math

import jax
import jax.numpy as jnp
from jax import lax
from jax.sharding import Mesh
from jax.sharding import PartitionSpec as P

BF16, F32 = jnp.bfloat16, jnp.float32
NAMES = ("zh", "y", "c", "x", "zl")
SIZES = (4, 4, 2, 4, 8)


def gelu_parts(v):
    cdf = 0.5 * (1.0 + jax.scipy.special.erf(v / math.sqrt(2.0)))
    return v * cdf, cdf + v * jnp.exp(-0.5 * v * v) / math.sqrt(2.0 * math.pi)


def gather(block, axis, size):
    return lax.all_to_all(jnp.broadcast_to(block[None], (size,) + block.shape), axis, 0, 0)


def scatter_sum(parts, axis):
    got = lax.all_to_all(parts, axis, 0, 0)
    return jnp.sum(got.astype(F32), axis=0)


def shards(layer_input, out_grad, norm_gain_vector, up_weight, down_weight):
    nzh, ny, nc, nx, nzl = SIZES
    rows, width = layer_input.shape
    hidden_width = up_weight.shape[1]
    part = width // (nzh * ny * nc)
    xf = layer_input.astype(F32)
    centered = xf - jnp.mean(xf, axis=1, keepdims=True)
    rstd = 1.0 / jnp.sqrt(jnp.mean(centered * centered, axis=1, keepdims=True) + 1e-06)
    xhat = centered * rstd
    normed = (xhat * norm_gain_vector).astype(BF16)

    pair = jnp.stack([normed, out_grad])
    pair = gather(pair, "zl", nzl)
    pair = pair.transpose(1, 0, 2, 3).reshape(2, nzl * rows, width)
    pair = gather(pair, "x", nx)
    normed_all = pair[:, 0].reshape(nx * nzl * rows, width)
    grad_all = pair[:, 1].reshape(nx * nzl * rows, width)

    pre = jnp.dot(normed_all, up_weight, preferred_element_type=F32)
    hidden_grad = jnp.einsum("td,fd->tf", grad_all, down_weight, preferred_element_type=F32)
    value, slope = gelu_parts(pre)
    hidden = value.astype(BF16)
    pre_grad = (hidden_grad * slope).astype(BF16)
    down_term = jnp.einsum("td,tf->df", grad_all, hidden, preferred_element_type=F32).astype(BF16)
    up_term = jnp.einsum("td,tf->df", normed_all, pre_grad, preferred_element_type=F32).astype(BF16)
    full_term = jnp.einsum("tf,df->td", pre_grad, up_weight, preferred_element_type=F32).astype(BF16)

    terms = jnp.stack([up_term, down_term]).reshape(2, nzh, ny, nc, part, hidden_width)
    terms = terms.transpose(3, 2, 1, 0, 4, 5)
    terms = scatter_sum(terms, "c").astype(BF16)
    terms = scatter_sum(terms, "y").astype(BF16)
    terms = scatter_sum(terms, "zh")
    up_grad, down_grad = terms[0], terms[1].T

    full_term = full_term.reshape(nx, nzl * rows, width)
    full_term = scatter_sum(full_term, "x").astype(BF16)
    normed_grad = scatter_sum(full_term.reshape(nzl, rows, width), "zl")

    g = normed_grad * norm_gain_vector
    back = rstd * (
        g
        - jnp.mean(g, axis=1, keepdims=True)
        - xhat * jnp.mean(g * xhat, axis=1, keepdims=True)
    )
    input_grad = (out_grad.astype(F32) + back).astype(BF16)
    return (input_grad, up_grad, down_grad)


def solution(mesh):
    fine = Mesh(mesh.devices.reshape(SIZES), NAMES)
    dp, mp, both = ("zh", "y", "c"), ("x", "zl"), NAMES
    return jax.shard_map(
        shards,
        mesh=fine,
        in_specs=(P(both, None), P(both, None), P(), P(None, mp), P(mp, None)),
        out_specs=(P(both, None), P(dp, mp), P(mp, dp)),
        check_vma=False,
    )
```

```python
import math

import jax
import jax.numpy as jnp
from jax import lax
from jax.sharding import Mesh
from jax.sharding import PartitionSpec as P

BF16, F32 = jnp.bfloat16, jnp.float32
NAMES = ("zh", "y", "c", "x", "zl")
SIZES = (4, 4, 2, 4, 8)
FAR = [(i, i ^ 4) for i in range(8)]
FOURS = [[0, 1, 2, 3], [4, 5, 6, 7]]
AROUND = [(2 * i + c, 2 * ((i + 1 - 2 * c) % 4) + c) for i in range(4) for c in range(2)]


def gelu_parts(v):
    cdf = 0.5 * (1.0 + jax.scipy.special.erf(v / math.sqrt(2.0)))
    return v * cdf, cdf + v * jnp.exp(-0.5 * v * v) / math.sqrt(2.0 * math.pi)


def copies(block, n):
    return jnp.broadcast_to(block[None], (n,) + block.shape)


def added(*terms):
    total = terms[0].astype(F32)
    for term in terms[1:]:
        total = total + term.astype(F32)
    return total


def pick(array, index, axis):
    return lax.dynamic_index_in_dim(array, index, axis, keepdims=False)


def shards(layer_input, out_grad, norm_gain_vector, up_weight, down_weight):
    nzh, ny, nc, nx, nzl = SIZES
    rows, width = layer_input.shape
    hidden_width = up_weight.shape[1]
    part = width // (nzh * ny * nc)
    zh, c = lax.axis_index("zh"), lax.axis_index("c")

    xf = layer_input.astype(F32)
    centered = xf - jnp.mean(xf, axis=1, keepdims=True)
    rstd = 1.0 / jnp.sqrt(jnp.mean(centered * centered, axis=1, keepdims=True) + 1e-06)
    xhat = centered * rstd
    normed = (xhat * norm_gain_vector).astype(BF16)

    pair = jnp.concatenate([normed, out_grad], axis=1)
    pair = jnp.concatenate([pair, lax.ppermute(pair, "zl", FAR)], axis=0)
    pair = lax.all_to_all(copies(pair, 4), "zl", 0, 0, axis_index_groups=FOURS)
    pair = pair.reshape(nzl * rows, 2 * width)
    pair = jnp.stack([pair[:, :width], pair[:, width:]])
    pair = lax.all_to_all(copies(pair, nx), "x", 0, 0)
    normed_all = pair[:, 0].reshape(nx * nzl * rows, width)
    grad_all = pair[:, 1].reshape(nx * nzl * rows, width)

    pre = jnp.dot(normed_all, up_weight, preferred_element_type=F32)
    value, slope = gelu_parts(pre)
    hidden = value.astype(BF16)
    hidden_grad = jnp.einsum("td,fd->tf", grad_all, down_weight, preferred_element_type=F32)
    pre_grad = (hidden_grad * slope).astype(BF16)

    def half(left, right):
        term = jnp.einsum("td,tf->df", left, right, preferred_element_type=F32).astype(BF16)
        term = term.reshape(nzh, ny, nc, part, hidden_width)
        got = lax.ppermute(pick(term, 1 - c, 2), "c", [(0, 1), (1, 0)])
        return added(pick(term, c, 2), got).astype(BF16).transpose(1, 0, 2, 3)

    terms = jnp.stack([half(grad_all, hidden), half(normed_all, pre_grad)], axis=2)
    terms = lax.all_to_all(terms, "y", 0, 0)
    terms = added(*[terms[i] for i in range(ny)]).astype(BF16)
    terms, pre_grad = lax.optimization_barrier((terms, pre_grad))

    step = 1 - 2 * c
    total = pick(terms, (zh - step) % nzh, 0)

    def hop(total, k, fence):
        got = lax.ppermute(total, ("zh", "c"), AROUND)
        got, fence = lax.optimization_barrier((got, fence))
        return added(got, pick(terms, (zh - k * step) % nzh, 0)), fence

    full_term = jnp.einsum("tf,df->td", pre_grad, up_weight, preferred_element_type=F32)
    full_term = full_term.astype(BF16).reshape(nx, nzl * rows, width)
    total, full_term = hop(total, 2, full_term)
    full_term = lax.all_to_all(full_term, "x", 0, 0)
    full_term = added(*[full_term[i] for i in range(nx)]).astype(BF16)
    total, full_term = hop(total.astype(BF16), 3, full_term)
    full_term = lax.all_to_all(
        full_term.reshape(4, 2 * rows, width), "zl", 0, 0, axis_index_groups=FOURS
    )
    full_term = added(*[full_term[i] for i in range(4)])
    far = lax.ppermute(full_term[rows:].astype(BF16), "zl", FAR)
    total, far = hop(total.astype(BF16), 4, far)
    normed_grad = added(full_term[:rows], far)
    up_grad, down_grad = total[1], total[0].T

    g = normed_grad * norm_gain_vector
    back = rstd * (
        g
        - jnp.mean(g, axis=1, keepdims=True)
        - xhat * jnp.mean(g * xhat, axis=1, keepdims=True)
    )
    input_grad = (out_grad.astype(F32) + back).astype(BF16)
    return (input_grad, up_grad, down_grad)


def solution(mesh):
    fine = Mesh(mesh.devices.reshape(SIZES), NAMES)
    dp, mp, both = ("zh", "y", "c"), ("x", "zl"), NAMES
    return jax.shard_map(
        shards,
        mesh=fine,
        in_specs=(P(both, None), P(both, None), P(), P(None, mp), P(mp, None)),
        out_specs=(P(both, None), P(dp, mp), P(mp, dp)),
        check_vma=False,
    )
```

```python
import math

import jax
import jax.numpy as jnp
from jax import lax
from jax.sharding import Mesh
from jax.sharding import PartitionSpec as P

BF16, F32 = jnp.bfloat16, jnp.float32
NAMES = ("zh", "y", "c", "x", "zl")
SIZES = (4, 4, 2, 4, 8)
AROUND = [(2 * i + c, 2 * ((i + 1 - 2 * c) % 4) + c) for i in range(4) for c in range(2)]


def gelu_parts(v):
    cdf = 0.5 * (1.0 + jax.scipy.special.erf(v / math.sqrt(2.0)))
    return v * cdf, cdf + v * jnp.exp(-0.5 * v * v) / math.sqrt(2.0 * math.pi)


def swap(block, distance):
    return lax.ppermute(block, "zl", [(i, i ^ distance) for i in range(8)])


def shift(block, distance):
    return lax.ppermute(block, "x", [(i, (i + distance) % 4) for i in range(4)])


def added(*terms):
    total = terms[0].astype(F32)
    for term in terms[1:]:
        total = total + term.astype(F32)
    return total


def pick(array, index, axis):
    return lax.dynamic_index_in_dim(array, index, axis, keepdims=False)


def shards(layer_input, out_grad, norm_gain_vector, up_weight, down_weight):
    nzh, ny, nc, nx, nzl = SIZES
    rows, width = layer_input.shape
    hidden_width = up_weight.shape[1]
    part = width // (nzh * ny * nc)
    zh, c = lax.axis_index("zh"), lax.axis_index("c")

    xf = layer_input.astype(F32)
    centered = xf - jnp.mean(xf, axis=1, keepdims=True)
    rstd = 1.0 / jnp.sqrt(jnp.mean(centered * centered, axis=1, keepdims=True) + 1e-06)
    xhat = centered * rstd
    normed = (xhat * norm_gain_vector).astype(BF16)

    def gathered(block):
        for distance in (4, 2, 1):
            block = jnp.concatenate([block, swap(block, distance)])
        left, right = shift(block, 1), shift(block, -1)
        middle = block.shape[0] // 2
        across = shift(left[:middle], 1), shift(right[middle:], -1)
        return jnp.concatenate([block, left, *across, right])

    grad_all, normed_all = gathered(out_grad), gathered(normed)

    pre = jnp.dot(normed_all, up_weight, preferred_element_type=F32)
    value, slope = gelu_parts(pre)
    hidden = value.astype(BF16)
    hidden_grad = jnp.einsum("td,fd->tf", grad_all, down_weight, preferred_element_type=F32)
    pre_grad = (hidden_grad * slope).astype(BF16)

    def half(left, right):
        term = jnp.einsum("td,tf->df", left, right, preferred_element_type=F32).astype(BF16)
        term = term.reshape(nzh, ny, nc, part, hidden_width)
        got = lax.ppermute(pick(term, 1 - c, 2), "c", [(0, 1), (1, 0)])
        return added(pick(term, c, 2), got).astype(BF16).transpose(1, 0, 2, 3)

    full_term = jnp.einsum("tf,df->td", pre_grad, up_weight, preferred_element_type=F32)
    full_term, pre_grad = lax.optimization_barrier((full_term.astype(BF16), pre_grad))
    own, left, across, right = jnp.split(full_term, nx)
    own = added(own, shift(left, -1), shift(across, 2), shift(right, 1))
    for distance in (1, 2, 4):
        middle = own.shape[0] // 2
        own = added(own[:middle], swap(own[middle:].astype(BF16), distance))
    normed_grad = own

    terms = jnp.stack([half(grad_all, hidden), half(normed_all, pre_grad)], axis=2)
    terms = lax.all_to_all(terms, "y", 0, 0)
    terms = added(*[terms[i] for i in range(ny)]).astype(BF16)

    step = 1 - 2 * c
    total = pick(terms, (zh - step) % nzh, 0)
    for hop in range(2, nzh + 1):
        got = lax.ppermute(total.astype(BF16), ("zh", "c"), AROUND)
        total = added(got, pick(terms, (zh - hop * step) % nzh, 0))
    up_grad, down_grad = total[1], total[0].T

    g = normed_grad * norm_gain_vector
    back = rstd * (
        g
        - jnp.mean(g, axis=1, keepdims=True)
        - xhat * jnp.mean(g * xhat, axis=1, keepdims=True)
    )
    input_grad = (out_grad.astype(F32) + back).astype(BF16)
    return (input_grad, up_grad, down_grad)


def solution(mesh):
    fine = Mesh(mesh.devices.reshape(SIZES), NAMES)
    dp, mp, both = ("zh", "y", "c"), ("x", "zl"), NAMES
    return jax.shard_map(
        shards,
        mesh=fine,
        in_specs=(P(both, None), P(both, None), P(), P(None, mp), P(mp, None)),
        out_specs=(P(both, None), P(dp, mp), P(mp, dp)),
        check_vma=False,
    )
```

```python
import math

import jax
import jax.numpy as jnp
from jax import lax
from jax.experimental import pallas as pl
from jax.experimental.pallas import tpu as pltpu
from jax.sharding import Mesh
from jax.sharding import PartitionSpec as P

BF16, F32 = jnp.bfloat16, jnp.float32
NAMES = ("zh", "y", "c", "x", "zl")
SIZES = (4, 4, 2, 4, 8)


def gelu_parts(v):
    cdf = 0.5 * (1.0 + jax.scipy.special.erf(v / math.sqrt(2.0)))
    return v * cdf, cdf + v * jnp.exp(-0.5 * v * v) / math.sqrt(2.0 * math.pi)


def swap(block, distance):
    return lax.ppermute(block, "zl", [(i, i ^ distance) for i in range(8)])


def shift(block, distance):
    return lax.ppermute(block, "x", [(i, (i + distance) % 4) for i in range(4)])


def pairs(axis, step):
    flip = {(c, s): 1 if c == s else 3 for c in range(2) for s in range(2)}
    if axis == "x":
        return ("c", "x"), [
            (4 * c + i, 4 * c + (i ^ flip[c, step])) for c in range(2) for i in range(4)
        ]
    return (axis, "c"), [
        (2 * i + c, 2 * (i ^ flip[c, step]) + c) for c in range(2) for i in range(4)
    ]


def paired(block, axis, step):
    names, moves = pairs(axis, step)
    return lax.ppermute(block, names, moves)


def place(own, other, c):
    apart = own ^ other
    odd = jnp.where(c == 0, (5 - apart) // 2, (apart + 1) // 2)
    return jnp.where(apart == 0, 0, jnp.where(apart == 2, 3, odd))


def added(*terms):
    total = terms[0].astype(F32)
    for term in terms[1:]:
        total = total + term.astype(F32)
    return total


def pick(array, index, axis):
    return lax.dynamic_index_in_dim(array, index, axis, keepdims=False)


def terms_kernel(where, grad, hidden, normed, pre_grad, keep, send):
    part = keep.shape[3]
    c = where[16]

    def block(g, _):
        columns = pl.ds(pl.multiple_of(g * 4 * part, 4 * part), 4 * part)
        at_z, there_z = where[4 + g // 2], where[12 + g // 2]
        for k, (left, right) in enumerate(((grad, hidden), (normed, pre_grad))):
            term = lax.dot_general(
                left[:, columns], right[...], (((0,), (0,)), ((), ())), preferred_element_type=F32
            ).astype(BF16)
            for pair in range(2):
                at_y = where[2 * (g % 2) + pair]
                there_y = where[8 + 2 * (g % 2) + pair]
                low = term[2 * pair * part : (2 * pair + 1) * part]
                high = term[(2 * pair + 1) * part : (2 * pair + 2) * part]

                @pl.when(c == 0)
                def _():
                    keep[at_y, at_z, k] = low
                    send[there_y, there_z, k] = high

                @pl.when(c == 1)
                def _():
                    keep[at_y, at_z, k] = high
                    send[there_y, there_z, k] = low

        return 0

    lax.fori_loop(0, 8, block, 0)


def term_halves(where, grad, hidden, normed, pre_grad):
    tokens, width = grad.shape
    hidden_width = hidden.shape[1]
    half = jax.ShapeDtypeStruct((4, 4, 2, width // 32, hidden_width), BF16)
    vmem = pl.BlockSpec(memory_space=pltpu.VMEM)
    return pl.pallas_call(
        terms_kernel,
        out_shape=(half, half),
        in_specs=[pl.BlockSpec(memory_space=pltpu.SMEM)] + [vmem] * 4,
        out_specs=(vmem, vmem),
        compiler_params=pltpu.CompilerParams(vmem_limit_bytes=32 * 1024 * 1024),
        cost_estimate=pl.CostEstimate(
            flops=4 * tokens * width * hidden_width,
            bytes_accessed=8 * width * hidden_width,
            transcendentals=0,
        ),
    )(where, grad, hidden, normed, pre_grad)


def shards(layer_input, out_grad, norm_gain_vector, up_weight, down_weight):
    nx, nzl = SIZES[3:]
    rows, width = layer_input.shape
    hidden_width = up_weight.shape[1]
    zh, y, c = lax.axis_index("zh"), lax.axis_index("y"), lax.axis_index("c")
    x, zl = lax.axis_index("x"), lax.axis_index("zl")

    xf = layer_input.astype(F32)
    centered = xf - jnp.mean(xf, axis=1, keepdims=True)
    rstd = 1.0 / jnp.sqrt(jnp.mean(centered * centered, axis=1, keepdims=True) + 1e-06)
    xhat = centered * rstd
    normed = (xhat * norm_gain_vector).astype(BF16)

    pair = jnp.stack([normed, out_grad])
    for distance in (4, 2, 1):
        pair = jnp.concatenate([pair, swap(pair, distance)], axis=1)
    middle = nzl * rows
    pair = lax.optimization_barrier(pair.reshape(2 * middle, width))
    left, right = shift(pair, 1), shift(pair, -1)
    across_normed, across_grad = shift(left[:middle], 1), shift(right[middle:], -1)
    normed_all = jnp.concatenate([pair[:middle], left[:middle], right[:middle], across_normed])
    grad_all = jnp.concatenate([pair[middle:], left[middle:], right[middle:], across_grad])

    pre = jnp.dot(normed_all, up_weight, preferred_element_type=F32)
    value, slope = gelu_parts(pre)
    hidden = value.astype(BF16)
    hidden_grad = jnp.einsum("td,fd->tf", grad_all, down_weight, preferred_element_type=F32)
    pre_grad = (hidden_grad * slope).astype(BF16)

    blocks = pre_grad.reshape(nx, middle, hidden_width)
    near, far = jnp.where(x % 2 == 0, 2, 1), jnp.where(x % 2 == 0, 1, 2)
    first, second = jnp.where(c == 0, near, far), jnp.where(c == 0, far, near)
    blocks = jnp.stack([blocks[0], pick(blocks, second, 0), pick(blocks, first, 0), blocks[3]])
    full_term = jnp.einsum("xtf,df->xtd", blocks, up_weight, preferred_element_type=F32)
    full_term = full_term.astype(BF16)
    x_first = paired(full_term[2:], "x", 0)
    x_second = paired(added(full_term[1], x_first[1]).astype(BF16), "x", 1)
    own = added(full_term[0], x_first[0], x_second)
    for distance in (1, 2, 4):
        half = own.shape[0] // 2
        own = added(own[:half], swap(own[half:].astype(BF16), distance))
    normed_grad = own


    four = jnp.arange(4)
    where = [place(own, four, core) for core in (c, 1 - c) for own in (y, zh)]
    where = jnp.concatenate(where + [c[None]]).astype(jnp.int32)
    keep, send = term_halves(where, grad_all, hidden, normed_all, pre_grad)
    core = lax.ppermute(send, "c", [(0, 1), (1, 0)])

    y_first = paired(added(keep[2:], core[2:]).astype(BF16), "y", 0)
    y_second = paired(added(keep[1], core[1], y_first[1]).astype(BF16), "y", 1)

    def summed(at):
        return added(keep[0, at], core[0, at], y_first[0, at], y_second[at])

    z_first = paired(summed(slice(2, 4)).astype(BF16), "zh", 0)
    z_second = paired(added(summed(1), z_first[1]).astype(BF16), "zh", 1)
    total = added(summed(0), z_first[0], z_second)
    down_grad, up_grad = total[0].T, total[1]

    g = normed_grad * norm_gain_vector
    back = rstd * (
        g
        - jnp.mean(g, axis=1, keepdims=True)
        - xhat * jnp.mean(g * xhat, axis=1, keepdims=True)
    )
    input_grad = (out_grad.astype(F32) + back).astype(BF16)
    return (input_grad, up_grad, down_grad)


def solution(mesh):
    fine = Mesh(mesh.devices.reshape(SIZES), NAMES)
    dp, mp, both = ("zh", "y", "c"), ("x", "zl"), NAMES
    return jax.shard_map(
        shards,
        mesh=fine,
        in_specs=(P(both, None), P(both, None), P(), P(None, mp), P(mp, None)),
        out_specs=(P(both, None), P(dp, mp), P(mp, dp)),
        check_vma=False,
    )
```

```python
import math

import jax
import jax.numpy as jnp
from jax import lax
from jax.experimental import pallas as pl
from jax.experimental.pallas import tpu as pltpu
from jax.sharding import Mesh
from jax.sharding import PartitionSpec as P

BF16, F32 = jnp.bfloat16, jnp.float32
NAMES = ("zh", "y", "c", "x", "zl")
SIZES = (4, 4, 2, 4, 8)


def gelu_parts(v):
    cdf = 0.5 * (1.0 + jax.scipy.special.erf(v / math.sqrt(2.0)))
    return v * cdf, cdf + v * jnp.exp(-0.5 * v * v) / math.sqrt(2.0 * math.pi)


def swap(block, distance):
    return lax.ppermute(block, "zl", [(i, i ^ distance) for i in range(8)])


def shift(block, distance):
    return lax.ppermute(block, "x", [(i, (i + distance) % 4) for i in range(4)])


def pairs(axis, step):
    flip = {(c, s): 1 if c == s else 3 for c in range(2) for s in range(2)}
    if axis == "x":
        return ("c", "x"), [
            (4 * c + i, 4 * c + (i ^ flip[c, step])) for c in range(2) for i in range(4)
        ]
    return (axis, "c"), [
        (2 * i + c, 2 * (i ^ flip[c, step]) + c) for c in range(2) for i in range(4)
    ]


def paired(block, axis, step):
    names, moves = pairs(axis, step)
    return lax.ppermute(block, names, moves)


def place(own, other, c):
    apart = own ^ other
    odd = jnp.where(c == 0, (5 - apart) // 2, (apart + 1) // 2)
    return jnp.where(apart == 0, 0, jnp.where(apart == 2, 3, odd))


def added(*terms):
    total = terms[0].astype(F32)
    for term in terms[1:]:
        total = total + term.astype(F32)
    return total


def pick(array, index, axis):
    return lax.dynamic_index_in_dim(array, index, axis, keepdims=False)


def term_kernel(where, left, right, keep, send):
    part = keep.shape[2]
    c = where[16]
    for g in range(8):
        columns = slice(4 * part * g, 4 * part * (g + 1))
        term = lax.dot_general(
            left[:, columns], right[...], (((0,), (0,)), ((), ())), preferred_element_type=F32
        ).astype(BF16)
        for pair in range(2):
            at_y, there_y = (where[at + 2 * (g % 2) + pair] for at in (0, 8))
            at_z, there_z = (where[at + g // 2] for at in (4, 12))
            low = term[2 * pair * part : (2 * pair + 1) * part]
            high = term[(2 * pair + 1) * part : (2 * pair + 2) * part]
            keep[at_y, at_z] = jnp.where(c == 0, low, high)
            send[there_y, there_z] = jnp.where(c == 0, high, low)


def term_halves(where, left, right):
    tokens, width = left.shape
    hidden_width = right.shape[1]
    half = jax.ShapeDtypeStruct((4, 4, width // 32, hidden_width), BF16)
    vmem = pl.BlockSpec(memory_space=pltpu.VMEM)
    return pl.pallas_call(
        term_kernel,
        out_shape=(half, half),
        in_specs=[pl.BlockSpec(memory_space=pltpu.SMEM), vmem, vmem],
        out_specs=(vmem, vmem),
        compiler_params=pltpu.CompilerParams(vmem_limit_bytes=12 * 1024 * 1024),
        cost_estimate=pl.CostEstimate(
            flops=2 * tokens * width * hidden_width,
            bytes_accessed=4 * width * hidden_width,
            transcendentals=0,
        ),
    )(where, left, right)


def shards(layer_input, out_grad, norm_gain_vector, up_weight, down_weight):
    nx, nzl = SIZES[3:]
    rows, width = layer_input.shape
    hidden_width = up_weight.shape[1]
    zh, y, c = lax.axis_index("zh"), lax.axis_index("y"), lax.axis_index("c")
    x, zl = lax.axis_index("x"), lax.axis_index("zl")

    xf = layer_input.astype(F32)
    centered = xf - jnp.mean(xf, axis=1, keepdims=True)
    rstd = 1.0 / jnp.sqrt(jnp.mean(centered * centered, axis=1, keepdims=True) + 1e-06)
    xhat = centered * rstd
    normed = (xhat * norm_gain_vector).astype(BF16)

    pair = jnp.stack([normed, out_grad])
    for distance in (4, 2, 1):
        pair = jnp.concatenate([pair, swap(pair, distance)], axis=1)
    middle = nzl * rows
    pair = lax.optimization_barrier(pair.reshape(2 * middle, width))
    left, right = shift(pair, 1), shift(pair, -1)
    across_normed, across_grad = shift(left[:middle], 1), shift(right[middle:], -1)
    normed_all = jnp.concatenate([pair[:middle], left[:middle], right[:middle], across_normed])
    grad_all = jnp.concatenate([pair[middle:], left[middle:], right[middle:], across_grad])

    pre = jnp.dot(normed_all, up_weight, preferred_element_type=F32)
    value, slope = gelu_parts(pre)
    hidden = value.astype(BF16)
    hidden_grad = jnp.einsum("td,fd->tf", grad_all, down_weight, preferred_element_type=F32)
    pre_grad = (hidden_grad * slope).astype(BF16)

    four = jnp.arange(4)
    where = [place(own, four, core) for core in (c, 1 - c) for own in (y, zh)]
    where = jnp.concatenate(where + [c[None]]).astype(jnp.int32)

    blocks = pre_grad.reshape(nx, middle, hidden_width)
    near, far = jnp.where(x % 2 == 0, 2, 1), jnp.where(x % 2 == 0, 1, 2)
    first, second = jnp.where(c == 0, near, far), jnp.where(c == 0, far, near)
    blocks = jnp.stack([blocks[0], pick(blocks, second, 0), pick(blocks, first, 0), blocks[3]])

    fence = lax.optimization_barrier
    down, up = term_halves(where, grad_all, hidden), term_halves(where, normed_all, pre_grad)

    def to_core(term):
        return lax.ppermute(term[1], "c", [(0, 1), (1, 0)])

    def to_y(term, core):
        return paired(added(term[0][2:], core[2:]).astype(BF16), "y", 0)

    def to_second_y(term, core, got):
        return paired(added(term[0][1], core[1], got[1]).astype(BF16), "y", 1)

    def summed(term, at):
        keep, core, got, second = term
        return added(keep[0, at], core[0, at], got[0, at], second[at])

    def to_z(*term):
        return paired(summed(term, slice(2, 4)).astype(BF16), "zh", 0)

    def to_second_z(term, got):
        return paired(added(summed(term, 1), got[1]).astype(BF16), "zh", 1)

    down_core, up_core = to_core(down), to_core(up)
    down_core, blocks = fence((down_core, blocks))
    full_term = jnp.einsum("xtf,df->xtd", blocks, up_weight, preferred_element_type=F32)
    full_term = full_term.astype(BF16)
    x_first = paired(full_term[2:], "x", 0)
    down_y, up_y = to_y(down, down_core), to_y(up, up_core)
    down_y, x_first = fence((down_y, x_first))
    x_second = paired(added(full_term[1], x_first[1]).astype(BF16), "x", 1)
    own = added(full_term[0], x_first[0], x_second)
    down_y2, up_y2 = to_second_y(down, down_core, down_y), to_second_y(up, up_core, up_y)
    down_y2, own = fence((down_y2, own))
    half = own.shape[0] // 2
    own = added(own[:half], swap(own[half:].astype(BF16), 1))
    down, up = (down[0], down_core, down_y, down_y2), (up[0], up_core, up_y, up_y2)
    down_z, up_z = to_z(*down), to_z(*up)
    down_z, own = fence((down_z, own))
    half = own.shape[0] // 2
    own = added(own[:half], swap(own[half:].astype(BF16), 2))
    down_z2, up_z2 = to_second_z(down, down_z), to_second_z(up, up_z)
    normed_grad = added(own[:rows], swap(own[rows:].astype(BF16), 4))
    down_grad = added(summed(down, 0), down_z[0], down_z2).T
    up_grad = added(summed(up, 0), up_z[0], up_z2)

    g = normed_grad * norm_gain_vector
    back = rstd * (
        g
        - jnp.mean(g, axis=1, keepdims=True)
        - xhat * jnp.mean(g * xhat, axis=1, keepdims=True)
    )
    input_grad = (out_grad.astype(F32) + back).astype(BF16)
    return (input_grad, up_grad, down_grad)


def solution(mesh):
    fine = Mesh(mesh.devices.reshape(SIZES), NAMES)
    dp, mp, both = ("zh", "y", "c"), ("x", "zl"), NAMES
    return jax.shard_map(
        shards,
        mesh=fine,
        in_specs=(P(both, None), P(both, None), P(), P(None, mp), P(mp, None)),
        out_specs=(P(both, None), P(dp, mp), P(mp, dp)),
        check_vma=False,
    )
```

```python
import math

import jax
import jax.numpy as jnp
from jax import lax
from jax.experimental import pallas as pl
from jax.experimental.pallas import tpu as pltpu
from jax.sharding import Mesh
from jax.sharding import PartitionSpec as P

BF16, F32 = jnp.bfloat16, jnp.float32
NAMES = ("zh", "y", "c", "x", "zl")
SIZES = (4, 4, 2, 4, 8)


def gelu_parts(v):
    cdf = 0.5 * (1.0 + jax.scipy.special.erf(v / math.sqrt(2.0)))
    return v * cdf, cdf + v * jnp.exp(-0.5 * v * v) / math.sqrt(2.0 * math.pi)


def swap(block, distance):
    return lax.ppermute(block, "zl", [(i, i ^ distance) for i in range(8)])


def shift(block, distance):
    return lax.ppermute(block, "x", [(i, (i + distance) % 4) for i in range(4)])


def pairs(axis, step):
    flip = {(c, s): 1 if c == s else 3 for c in range(2) for s in range(2)}
    if axis == "x":
        return ("c", "x"), [
            (4 * c + i, 4 * c + (i ^ flip[c, step])) for c in range(2) for i in range(4)
        ]
    return (axis, "c"), [
        (2 * i + c, 2 * (i ^ flip[c, step]) + c) for c in range(2) for i in range(4)
    ]


def paired(block, axis, step):
    names, moves = pairs(axis, step)
    return lax.ppermute(block, names, moves)


def place(own, other, c):
    apart = own ^ other
    odd = jnp.where(c == 0, (5 - apart) // 2, (apart + 1) // 2)
    return jnp.where(apart == 0, 0, jnp.where(apart == 2, 3, odd))


def added(*terms):
    total = terms[0].astype(F32)
    for term in terms[1:]:
        total = total + term.astype(F32)
    return total


def pick(array, index, axis):
    return lax.dynamic_index_in_dim(array, index, axis, keepdims=False)


def pack_kernel(layer_input, out_grad, gain, packed, stats):
    rows, width = layer_input.shape
    xf = layer_input[...].astype(F32)
    mean = jnp.mean(xf, axis=1, keepdims=True)
    centered = xf - mean
    rstd = 1.0 / jnp.sqrt(jnp.mean(centered * centered, axis=1, keepdims=True) + 1e-06)
    normed = (centered * rstd * gain[...]).astype(BF16)
    half = width // 2
    for at, block in enumerate((normed, out_grad[...])):
        packed[2 * at * rows : (2 * at + 1) * rows] = block[:, :half]
        packed[(2 * at + 1) * rows : (2 * at + 2) * rows] = block[:, half:]
    stats[:, 0:1] = mean
    stats[:, 1:2] = rstd


def unpack_kernel(own, far, block):
    rows, half = own.shape[0] // 4, own.shape[1]
    for at in range(2):
        for k, source in enumerate((own, far)):
            to = slice((2 * at + k) * rows, (2 * at + k + 1) * rows)
            block[to, :half] = source[2 * at * rows : (2 * at + 1) * rows]
            block[to, half:] = source[(2 * at + 1) * rows : (2 * at + 2) * rows]


def join_kernel(*refs):
    pieces, outs = refs[:4], refs[4:]
    rows = pieces[0].shape[0] // 2
    for k, piece in enumerate(pieces):
        for at, out in enumerate(outs):
            out[k * rows : (k + 1) * rows] = piece[at * rows : (at + 1) * rows]


def in_vmem(kernel, outs, *operands):
    return pl.pallas_call(
        kernel,
        out_shape=[jax.ShapeDtypeStruct(*out) for out in outs],
        in_specs=[pl.BlockSpec(memory_space=pltpu.VMEM)] * len(operands),
        out_specs=[pl.BlockSpec(memory_space=pltpu.VMEM)] * len(outs),
        compiler_params=pltpu.CompilerParams(vmem_limit_bytes=8 * 1024 * 1024),
    )(*operands)


def term_kernel(where, left, right, keep, send):
    part = keep.shape[2]
    c = where[16]
    for g in range(8):
        columns = slice(4 * part * g, 4 * part * (g + 1))
        term = lax.dot_general(
            left[:, columns], right[...], (((0,), (0,)), ((), ())), preferred_element_type=F32
        ).astype(BF16)
        for pair in range(2):
            at_y, there_y = (where[at + 2 * (g % 2) + pair] for at in (0, 8))
            at_z, there_z = (where[at + g // 2] for at in (4, 12))
            low = term[2 * pair * part : (2 * pair + 1) * part]
            high = term[(2 * pair + 1) * part : (2 * pair + 2) * part]
            keep[at_y, at_z] = jnp.where(c == 0, low, high)
            send[there_y, there_z] = jnp.where(c == 0, high, low)


def term_halves(where, left, right):
    tokens, width = left.shape
    hidden_width = right.shape[1]
    half = jax.ShapeDtypeStruct((4, 4, width // 32, hidden_width), BF16)
    vmem = pl.BlockSpec(memory_space=pltpu.VMEM)
    return pl.pallas_call(
        term_kernel,
        out_shape=(half, half),
        in_specs=[pl.BlockSpec(memory_space=pltpu.SMEM), vmem, vmem],
        out_specs=(vmem, vmem),
        compiler_params=pltpu.CompilerParams(vmem_limit_bytes=12 * 1024 * 1024),
        cost_estimate=pl.CostEstimate(
            flops=2 * tokens * width * hidden_width,
            bytes_accessed=4 * width * hidden_width,
            transcendentals=0,
        ),
    )(where, left, right)


def shards(layer_input, out_grad, norm_gain_vector, up_weight, down_weight):
    nx, nzl = SIZES[3:]
    rows, width = layer_input.shape
    hidden_width = up_weight.shape[1]
    zh, y, c = lax.axis_index("zh"), lax.axis_index("y"), lax.axis_index("c")
    x, zl = lax.axis_index("x"), lax.axis_index("zl")

    packed, stats = in_vmem(
        pack_kernel,
        [((4 * rows, width // 2), BF16), ((rows, 2), F32)],
        layer_input,
        out_grad,
        norm_gain_vector[None],
    )
    (block,) = in_vmem(unpack_kernel, [((4 * rows, width), BF16)], packed, swap(packed, 4))
    middle = nzl * rows
    normed, grad = in_vmem(
        join_kernel, [((middle, width), BF16)] * 2, block, *[swap(block, k) for k in (1, 2, 3)]
    )
    normed_left, grad_right = shift(normed, 1), shift(grad, -1)
    grad_left, normed_right = shift(grad, 1), shift(normed, -1)
    normed_all = jnp.concatenate([normed, normed_left, normed_right, shift(normed_left, 1)])
    grad_all = jnp.concatenate([grad, grad_left, grad_right, shift(grad_right, -1)])

    pre = jnp.dot(normed_all, up_weight, preferred_element_type=F32)
    value, slope = gelu_parts(pre)
    hidden = value.astype(BF16)
    hidden_grad = jnp.einsum("td,fd->tf", grad_all, down_weight, preferred_element_type=F32)
    pre_grad = (hidden_grad * slope).astype(BF16)

    four = jnp.arange(4)
    where = [place(own, four, core) for core in (c, 1 - c) for own in (y, zh)]
    where = jnp.concatenate(where + [c[None]]).astype(jnp.int32)

    blocks = pre_grad.reshape(nx, middle, hidden_width)
    near, far = jnp.where(x % 2 == 0, 2, 1), jnp.where(x % 2 == 0, 1, 2)
    first, second = jnp.where(c == 0, near, far), jnp.where(c == 0, far, near)
    blocks = jnp.stack([blocks[0], pick(blocks, second, 0), pick(blocks, first, 0), blocks[3]])

    fence = lax.optimization_barrier
    down, up = term_halves(where, grad_all, hidden), term_halves(where, normed_all, pre_grad)

    def to_core(term):
        return lax.ppermute(term[1], "c", [(0, 1), (1, 0)])

    def to_y(term, core):
        return paired(added(term[0][2:], core[2:]).astype(BF16), "y", 0)

    def to_second_y(term, core, got):
        return paired(added(term[0][1], core[1], got[1]).astype(BF16), "y", 1)

    def summed(term, at):
        keep, core, got, second = term
        return added(keep[0, at], core[0, at], got[0, at], second[at])

    def to_z(*term):
        return paired(summed(term, slice(2, 4)).astype(BF16), "zh", 0)

    def to_second_z(term, got):
        return paired(added(summed(term, 1), got[1]).astype(BF16), "zh", 1)

    down_core, up_core = to_core(down), to_core(up)
    down_core, blocks = fence((down_core, blocks))
    full_term = jnp.einsum("xtf,df->xtd", blocks, up_weight, preferred_element_type=F32)
    full_term = full_term.astype(BF16)
    x_first = paired(full_term[2:], "x", 0)
    down_y, up_y = to_y(down, down_core), to_y(up, up_core)
    down_y, x_first = fence((down_y, x_first))
    x_second = paired(added(full_term[1], x_first[1]).astype(BF16), "x", 1)
    own = added(full_term[0], x_first[0], x_second)
    down_y2, up_y2 = to_second_y(down, down_core, down_y), to_second_y(up, up_core, up_y)
    down_y2, own = fence((down_y2, own))
    half = own.shape[0] // 2
    own = added(own[:half], swap(own[half:].astype(BF16), 2))
    down, up = (down[0], down_core, down_y, down_y2), (up[0], up_core, up_y, up_y2)
    down_z, up_z = to_z(*down), to_z(*up)
    down_z, own = fence((down_z, own))
    half = own.shape[0] // 2
    own = added(own[:half], swap(own[half:].astype(BF16), 1))
    down_z2, up_z2 = to_second_z(down, down_z), to_second_z(up, up_z)
    normed_grad = added(own[:rows], swap(own[rows:].astype(BF16), 4))
    down_grad = added(summed(down, 0), down_z[0], down_z2).T
    up_grad = added(summed(up, 0), up_z[0], up_z2)

    rstd = stats[:, 1:2]
    xhat = (layer_input.astype(F32) - stats[:, 0:1]) * rstd
    g = normed_grad * norm_gain_vector
    back = rstd * (
        g
        - jnp.mean(g, axis=1, keepdims=True)
        - xhat * jnp.mean(g * xhat, axis=1, keepdims=True)
    )
    input_grad = (out_grad.astype(F32) + back).astype(BF16)
    return (input_grad, up_grad, down_grad)


def solution(mesh):
    fine = Mesh(mesh.devices.reshape(SIZES), NAMES)
    dp, mp, both = ("zh", "y", "c"), ("x", "zl"), NAMES
    return jax.shard_map(
        shards,
        mesh=fine,
        in_specs=(P(both, None), P(both, None), P(), P(None, mp), P(mp, None)),
        out_specs=(P(both, None), P(dp, mp), P(mp, dp)),
        check_vma=False,
    )
```

```python
import math

import jax
import jax.numpy as jnp
from jax import lax
from jax.experimental import pallas as pl
from jax.experimental.pallas import tpu as pltpu
from jax.sharding import Mesh
from jax.sharding import PartitionSpec as P

BF16, F32 = jnp.bfloat16, jnp.float32
NAMES = ("zh", "y", "c", "x", "zl")
SIZES = (4, 4, 2, 4, 8)


def gelu_parts(v):
    cdf = 0.5 * (1.0 + jax.scipy.special.erf(v / math.sqrt(2.0)))
    return v * cdf, cdf + v * jnp.exp(-0.5 * v * v) / math.sqrt(2.0 * math.pi)


def swap(block, distance):
    return lax.ppermute(block, "zl", [(i, i ^ distance) for i in range(8)])


def x_moves(way):
    moves = [(4 * c + i, 4 * c + (i + way * (1 - 2 * c)) % 4) for c in range(2) for i in range(4)]
    return lambda block: lax.ppermute(block, ("c", "x"), moves)


def pairs(axis, step):
    flip = {(c, s): 1 if c == s else 3 for c in range(2) for s in range(2)}
    if axis == "x":
        return ("c", "x"), [
            (4 * c + i, 4 * c + (i ^ flip[c, step])) for c in range(2) for i in range(4)
        ]
    return (axis, "c"), [
        (2 * i + c, 2 * (i ^ flip[c, step]) + c) for c in range(2) for i in range(4)
    ]


def paired(block, axis, step):
    names, moves = pairs(axis, step)
    return lax.ppermute(block, names, moves)


def place(own, other, c):
    apart = own ^ other
    odd = jnp.where(c == 0, (5 - apart) // 2, (apart + 1) // 2)
    return jnp.where(apart == 0, 0, jnp.where(apart == 2, 3, odd))


def added(*terms):
    total = terms[0].astype(F32)
    for term in terms[1:]:
        total = total + term.astype(F32)
    return total


def pick(array, index, axis):
    return lax.dynamic_index_in_dim(array, index, axis, keepdims=False)


def pack_kernel(layer_input, out_grad, gain, packed, stats, rows_in, grad_in, gain_in, sems):
    loads = [
        pltpu.make_async_copy(source, target, sems.at[k])
        for k, (source, target) in enumerate(
            ((layer_input, rows_in), (gain, gain_in), (out_grad, grad_in))
        )
    ]
    for load in loads:
        load.start()
    rows, width = rows_in.shape
    half = width // 2
    loads[0].wait()
    xf = rows_in[...].astype(F32)
    mean = jnp.mean(xf, axis=1, keepdims=True)
    centered = xf - mean
    rstd = 1.0 / jnp.sqrt(jnp.mean(centered * centered, axis=1, keepdims=True) + 1e-06)
    loads[1].wait()
    normed = (centered * rstd * gain_in[...]).astype(BF16)
    loads[2].wait()
    for at, block in enumerate((normed, grad_in[...])):
        packed[2 * at * rows : (2 * at + 1) * rows] = block[:, :half]
        packed[(2 * at + 1) * rows : (2 * at + 2) * rows] = block[:, half:]
    stats[:, 0:1] = mean
    stats[:, 1:2] = rstd


def pack(layer_input, out_grad, gain):
    rows, width = layer_input.shape
    vmem = pl.BlockSpec(memory_space=pltpu.VMEM)
    return pl.pallas_call(
        pack_kernel,
        out_shape=(
            jax.ShapeDtypeStruct((4 * rows, width // 2), BF16),
            jax.ShapeDtypeStruct((rows, 2), F32),
        ),
        in_specs=[pl.BlockSpec(memory_space=pl.ANY)] * 3,
        out_specs=(vmem, vmem),
        scratch_shapes=[
            pltpu.VMEM((rows, width), BF16),
            pltpu.VMEM((rows, width), BF16),
            pltpu.VMEM((1, width), F32),
            pltpu.SemaphoreType.DMA((3,)),
        ],
        compiler_params=pltpu.CompilerParams(vmem_limit_bytes=4 * 1024 * 1024),
    )(layer_input, out_grad, gain[None])


def unpack_kernel(own, far, block):
    rows, half = own.shape[0] // 4, own.shape[1]
    for at in range(2):
        for k, source in enumerate((own, far)):
            to = slice((2 * at + k) * rows, (2 * at + k + 1) * rows)
            block[to, :half] = source[2 * at * rows : (2 * at + 1) * rows]
            block[to, half:] = source[(2 * at + 1) * rows : (2 * at + 2) * rows]


def join_kernel(*refs):
    pieces, outs = refs[:4], refs[4:]
    rows = pieces[0].shape[0] // 2
    for k, piece in enumerate(pieces):
        for at, out in enumerate(outs):
            out[k * rows : (k + 1) * rows] = piece[at * rows : (at + 1) * rows]


def in_vmem(kernel, outs, *operands):
    return pl.pallas_call(
        kernel,
        out_shape=[jax.ShapeDtypeStruct(*out) for out in outs],
        in_specs=[pl.BlockSpec(memory_space=pltpu.VMEM)] * len(operands),
        out_specs=[pl.BlockSpec(memory_space=pltpu.VMEM)] * len(outs),
        compiler_params=pltpu.CompilerParams(vmem_limit_bytes=8 * 1024 * 1024),
    )(*operands)


def pre_kernel(*refs):
    pieces, (weight, rows, hidden, slope) = refs[:4], refs[4:]
    count = pieces[0].shape[0]
    for k, piece in enumerate(pieces):
        rows[k * count : (k + 1) * count] = piece[...]
    pre = jnp.dot(rows[...], weight[...], preferred_element_type=F32)
    value, slope[...] = gelu_parts(pre)
    hidden[...] = value.astype(BF16)


def write_halves(where, left, right, keep, send):
    part = keep.shape[2]
    c = where[16]
    for g in range(8):
        columns = slice(4 * part * g, 4 * part * (g + 1))
        term = lax.dot_general(
            left[:, columns], right, (((0,), (0,)), ((), ())), preferred_element_type=F32
        ).astype(BF16)
        for pair in range(2):
            at_y, there_y = (where[at + 2 * (g % 2) + pair] for at in (0, 8))
            at_z, there_z = (where[at + g // 2] for at in (4, 12))
            low = term[2 * pair * part : (2 * pair + 1) * part]
            high = term[(2 * pair + 1) * part : (2 * pair + 2) * part]
            keep[at_y, at_z] = jnp.where(c == 0, low, high)
            send[there_y, there_z] = jnp.where(c == 0, high, low)


def down_kernel(where, *refs):
    pieces, (hidden, rows, keep, send) = refs[:4], refs[4:]
    count = pieces[0].shape[0]
    for k, piece in enumerate(pieces):
        rows[k * count : (k + 1) * count] = piece[...]
    write_halves(where, rows, hidden[...], keep, send)


def up_kernel(where, grad, normed, slope, weight, pre_grad, keep, send):
    hidden_grad = lax.dot_general(
        grad[...], weight[...], (((1,), (1,)), ((), ())), preferred_element_type=F32
    )
    product = (hidden_grad * slope[...]).astype(BF16)
    pre_grad[...] = product
    write_halves(where, normed, product, keep, send)


def computed(kernel, flops, outs, *operands):
    vmem = pl.BlockSpec(memory_space=pltpu.VMEM)
    scalars = [operand.dtype == jnp.int32 for operand in operands]
    return pl.pallas_call(
        kernel,
        out_shape=[jax.ShapeDtypeStruct(*out) for out in outs],
        in_specs=[pl.BlockSpec(memory_space=pltpu.SMEM) if scalar else vmem for scalar in scalars],
        out_specs=[vmem] * len(outs),
        compiler_params=pltpu.CompilerParams(vmem_limit_bytes=12 * 1024 * 1024),
        cost_estimate=pl.CostEstimate(
            flops=flops, bytes_accessed=8 * 1024 * 1024, transcendentals=0
        ),
    )(*operands)


def shards(layer_input, out_grad, norm_gain_vector, up_weight, down_weight):
    nx, nzl = SIZES[3:]
    rows, width = layer_input.shape
    hidden_width = up_weight.shape[1]
    zh, y, c = lax.axis_index("zh"), lax.axis_index("y"), lax.axis_index("c")
    x, zl = lax.axis_index("x"), lax.axis_index("zl")

    packed, stats = pack(layer_input, out_grad, norm_gain_vector)
    (block,) = in_vmem(unpack_kernel, [((4 * rows, width), BF16)], packed, swap(packed, 4))
    middle = nzl * rows
    normed, grad = in_vmem(
        join_kernel, [((middle, width), BF16)] * 2, block, *[swap(block, k) for k in (1, 2, 3)]
    )
    ahead, back = x_moves(1), x_moves(-1)
    normed_ahead, grad_ahead = ahead(normed), ahead(grad)
    normed_pieces = normed, normed_ahead, back(normed), ahead(normed_ahead)
    grad_pieces = grad, grad_ahead, back(grad), ahead(grad_ahead)

    four = jnp.arange(4)
    where = [place(own, four, core) for core in (c, 1 - c) for own in (y, zh)]
    where = jnp.concatenate(where + [c[None]]).astype(jnp.int32)

    tokens = nx * middle
    shape = (tokens, hidden_width)
    flops = 2 * tokens * width * hidden_width
    halves = [((4, 4, width // 32, hidden_width), BF16)] * 2
    rows_of = ((tokens, width), BF16)
    normed_all, hidden, slope = computed(
        pre_kernel, flops, [rows_of, (shape, BF16), (shape, F32)], *normed_pieces, up_weight
    )
    grad_all, *down = computed(down_kernel, flops, [rows_of] + halves, where, *grad_pieces, hidden)
    pre_grad, *up = computed(
        up_kernel, 2 * flops, [(shape, BF16)] + halves, where, grad_all, normed_all, slope, down_weight
    )

    blocks = pre_grad.reshape(nx, middle, hidden_width)
    first, second = jnp.where(x % 2 == 0, 2, 1), jnp.where(x % 2 == 0, 1, 2)
    blocks = jnp.stack([blocks[0], pick(blocks, second, 0), pick(blocks, first, 0), blocks[3]])

    fence = lax.optimization_barrier

    def to_core(term):
        return lax.ppermute(term[1], "c", [(0, 1), (1, 0)])

    def to_y(term, core):
        return paired(added(term[0][2:], core[2:]).astype(BF16), "y", 0)

    def to_second_y(term, core, got):
        return paired(added(term[0][1], core[1], got[1]).astype(BF16), "y", 1)

    def summed(term, at):
        keep, core, got, second = term
        return added(keep[0, at], core[0, at], got[0, at], second[at])

    def to_z(*term):
        return paired(summed(term, slice(2, 4)).astype(BF16), "zh", 0)

    def to_second_z(term, got):
        return paired(added(summed(term, 1), got[1]).astype(BF16), "zh", 1)

    up_core, down_core = to_core(up), to_core(down)
    up_core, blocks = fence((up_core, blocks))
    full_term = jnp.einsum("xtf,df->xtd", blocks, up_weight, preferred_element_type=F32)
    full_term = full_term.astype(BF16)
    x_first = paired(full_term[2:], "x", 0)
    up_y, down_y = to_y(up, up_core), to_y(down, down_core)
    up_y, x_first = fence((up_y, x_first))
    x_second = paired(added(full_term[1], x_first[1]).astype(BF16), "x", 1)
    own = added(full_term[0], x_first[0], x_second)
    up_y2, down_y2 = to_second_y(up, up_core, up_y), to_second_y(down, down_core, down_y)
    up_y2, own = fence((up_y2, own))
    half = own.shape[0] // 2
    own = added(own[:half], swap(own[half:].astype(BF16), 2))
    up, down = (up[0], up_core, up_y, up_y2), (down[0], down_core, down_y, down_y2)
    up_z, down_z = to_z(*up), to_z(*down)
    up_z, own = fence((up_z, own))
    half = own.shape[0] // 2
    own = added(own[:half], swap(own[half:].astype(BF16), 1))
    up_z2, down_z2 = to_second_z(up, up_z), to_second_z(down, down_z)
    normed_grad = added(own[:rows], swap(own[rows:].astype(BF16), 4))
    down_grad = added(summed(down, 0), down_z[0], down_z2).T
    up_grad = added(summed(up, 0), up_z[0], up_z2)

    rstd = stats[:, 1:2]
    xhat = (layer_input.astype(F32) - stats[:, 0:1]) * rstd
    g = normed_grad * norm_gain_vector
    back = rstd * (
        g
        - jnp.mean(g, axis=1, keepdims=True)
        - xhat * jnp.mean(g * xhat, axis=1, keepdims=True)
    )
    input_grad = (out_grad.astype(F32) + back).astype(BF16)
    return (input_grad, up_grad, down_grad)


def solution(mesh):
    fine = Mesh(mesh.devices.reshape(SIZES), NAMES)
    dp, mp, both = ("zh", "y", "c"), ("x", "zl"), NAMES
    return jax.shard_map(
        shards,
        mesh=fine,
        in_specs=(P(both, None), P(both, None), P(), P(None, mp), P(mp, None)),
        out_specs=(P(both, None), P(dp, mp), P(mp, dp)),
        check_vma=False,
    )
```

```python
import math

import jax
import jax.numpy as jnp
from jax import lax
from jax.experimental import pallas as pl
from jax.experimental.pallas import tpu as pltpu
from jax.sharding import Mesh
from jax.sharding import PartitionSpec as P

BF16, F32 = jnp.bfloat16, jnp.float32
NAMES = ("zh", "y", "c", "x", "zl")
SIZES = (4, 4, 2, 4, 8)


def gelu_parts(v):
    cdf = 0.5 * (1.0 + jax.scipy.special.erf(v / math.sqrt(2.0)))
    return v * cdf, cdf + v * jnp.exp(-0.5 * v * v) / math.sqrt(2.0 * math.pi)


def swap(block, distance):
    return lax.ppermute(block, "zl", [(i, i ^ distance) for i in range(8)])


def x_moves(way):
    moves = [(4 * c + i, 4 * c + (i + way * (1 - 2 * c)) % 4) for c in range(2) for i in range(4)]
    return lambda block: lax.ppermute(block, ("c", "x"), moves)


def pairs(axis, step):
    flip = {(c, s): 1 if c == s else 3 for c in range(2) for s in range(2)}
    if axis == "x":
        return ("c", "x"), [
            (4 * c + i, 4 * c + (i ^ flip[c, step])) for c in range(2) for i in range(4)
        ]
    return (axis, "c"), [
        (2 * i + c, 2 * (i ^ flip[c, step]) + c) for c in range(2) for i in range(4)
    ]


def paired(block, axis, step):
    names, moves = pairs(axis, step)
    return lax.ppermute(block, names, moves)


def place(own, other, c):
    apart = own ^ other
    odd = jnp.where(c == 0, (5 - apart) // 2, (apart + 1) // 2)
    return jnp.where(apart == 0, 0, jnp.where(apart == 2, 3, odd))


def added(*terms):
    total = terms[0].astype(F32)
    for term in terms[1:]:
        total = total + term.astype(F32)
    return total


def pick(array, index, axis):
    return lax.dynamic_index_in_dim(array, index, axis, keepdims=False)


def pack_kernel(layer_input, out_grad, gain, packed, stats, rows_in, grad_in, gain_in, sems):
    loads = [
        pltpu.make_async_copy(source, target, sems.at[k])
        for k, (source, target) in enumerate(
            ((layer_input, rows_in), (gain, gain_in), (out_grad, grad_in))
        )
    ]
    for load in loads:
        load.start()
    rows, width = rows_in.shape
    half = width // 2
    loads[0].wait()
    xf = rows_in[...].astype(F32)
    mean = jnp.mean(xf, axis=1, keepdims=True)
    centered = xf - mean
    rstd = 1.0 / jnp.sqrt(jnp.mean(centered * centered, axis=1, keepdims=True) + 1e-06)
    loads[1].wait()
    normed = (centered * rstd * gain_in[...]).astype(BF16)
    loads[2].wait()
    for at, block in enumerate((normed, grad_in[...])):
        packed[2 * at * rows : (2 * at + 1) * rows] = block[:, :half]
        packed[(2 * at + 1) * rows : (2 * at + 2) * rows] = block[:, half:]
    stats[:, 0:1] = mean
    stats[:, 1:2] = rstd


def pack(layer_input, out_grad, gain):
    rows, width = layer_input.shape
    vmem = pl.BlockSpec(memory_space=pltpu.VMEM)
    return pl.pallas_call(
        pack_kernel,
        out_shape=(
            jax.ShapeDtypeStruct((4 * rows, width // 2), BF16),
            jax.ShapeDtypeStruct((rows, 2), F32),
        ),
        in_specs=[pl.BlockSpec(memory_space=pl.ANY)] * 3,
        out_specs=(vmem, vmem),
        scratch_shapes=[
            pltpu.VMEM((rows, width), BF16),
            pltpu.VMEM((rows, width), BF16),
            pltpu.VMEM((1, width), F32),
            pltpu.SemaphoreType.DMA((3,)),
        ],
        compiler_params=pltpu.CompilerParams(vmem_limit_bytes=4 * 1024 * 1024),
    )(layer_input, out_grad, gain[None])


def unpack_kernel(own, far, block):
    rows, half = own.shape[0] // 4, own.shape[1]
    for at in range(2):
        for k, source in enumerate((own, far)):
            to = slice((2 * at + k) * rows, (2 * at + k + 1) * rows)
            block[to, :half] = source[2 * at * rows : (2 * at + 1) * rows]
            block[to, half:] = source[(2 * at + 1) * rows : (2 * at + 2) * rows]


def join_kernel(*refs):
    pieces, outs = refs[:4], refs[4:]
    rows = pieces[0].shape[0] // 2
    for k, piece in enumerate(pieces):
        for at, out in enumerate(outs):
            out[k * rows : (k + 1) * rows] = piece[at * rows : (at + 1) * rows]


def in_vmem(kernel, outs, *operands):
    return pl.pallas_call(
        kernel,
        out_shape=[jax.ShapeDtypeStruct(*out) for out in outs],
        in_specs=[pl.BlockSpec(memory_space=pltpu.VMEM)] * len(operands),
        out_specs=[pl.BlockSpec(memory_space=pltpu.VMEM)] * len(outs),
        compiler_params=pltpu.CompilerParams(vmem_limit_bytes=8 * 1024 * 1024),
    )(*operands)


def pre_kernel(*refs):
    pieces, (weight, rows, hidden, slope) = refs[:4], refs[4:]
    count = pieces[0].shape[0]
    for k, piece in enumerate(pieces):
        rows[k * count : (k + 1) * count] = piece[...]
    pre = jnp.dot(rows[...], weight[...], preferred_element_type=F32)
    value, slope[...] = gelu_parts(pre)
    hidden[...] = value.astype(BF16)


def write_halves(where, left, right, keep, send):
    part = keep.shape[2]
    c = where[16]
    for g in range(8):
        columns = slice(4 * part * g, 4 * part * (g + 1))
        term = lax.dot_general(
            left[:, columns], right, (((0,), (0,)), ((), ())), preferred_element_type=F32
        ).astype(BF16)
        for pair in range(2):
            at_y, there_y = (where[at + 2 * (g % 2) + pair] for at in (0, 8))
            at_z, there_z = (where[at + g // 2] for at in (4, 12))
            low = term[2 * pair * part : (2 * pair + 1) * part]
            high = term[(2 * pair + 1) * part : (2 * pair + 2) * part]
            keep[at_y, at_z] = jnp.where(c == 0, low, high)
            send[there_y, there_z] = jnp.where(c == 0, high, low)


def down_kernel(where, *refs):
    pieces, (hidden, rows, keep, send) = refs[:4], refs[4:]
    count = pieces[0].shape[0]
    for k, piece in enumerate(pieces):
        rows[k * count : (k + 1) * count] = piece[...]
    write_halves(where, rows, hidden[...], keep, send)


def up_kernel(where, grad, normed, slope, weight, pre_grad, keep, send):
    hidden_grad = lax.dot_general(
        grad[...], weight[...], (((1,), (1,)), ((), ())), preferred_element_type=F32
    )
    product = (hidden_grad * slope[...]).astype(BF16)
    pre_grad[...] = product
    write_halves(where, normed, product, keep, send)


def computed(kernel, flops, outs, *operands):
    vmem = pl.BlockSpec(memory_space=pltpu.VMEM)
    scalars = [operand.dtype == jnp.int32 for operand in operands]
    return pl.pallas_call(
        kernel,
        out_shape=[jax.ShapeDtypeStruct(*out) for out in outs],
        in_specs=[pl.BlockSpec(memory_space=pltpu.SMEM) if scalar else vmem for scalar in scalars],
        out_specs=[vmem] * len(outs),
        compiler_params=pltpu.CompilerParams(vmem_limit_bytes=12 * 1024 * 1024),
        cost_estimate=pl.CostEstimate(
            flops=flops, bytes_accessed=8 * 1024 * 1024, transcendentals=0
        ),
    )(*operands)


def shards(layer_input, out_grad, norm_gain_vector, up_weight, down_weight):
    nx, nzl = SIZES[3:]
    rows, width = layer_input.shape
    hidden_width = up_weight.shape[1]
    zh, y, c = lax.axis_index("zh"), lax.axis_index("y"), lax.axis_index("c")
    x, zl = lax.axis_index("x"), lax.axis_index("zl")

    packed, stats = pack(layer_input, out_grad, norm_gain_vector)
    (block,) = in_vmem(unpack_kernel, [((4 * rows, width), BF16)], packed, swap(packed, 4))
    middle = nzl * rows
    normed, grad = in_vmem(
        join_kernel, [((middle, width), BF16)] * 2, block, *[swap(block, k) for k in (2, 1, 3)]
    )
    ahead, back = x_moves(1), x_moves(-1)
    normed_ahead, grad_ahead = ahead(normed), ahead(grad)
    normed_pieces = normed, normed_ahead, back(normed), ahead(normed_ahead)
    grad_pieces = grad, grad_ahead, back(grad), ahead(grad_ahead)

    four = jnp.arange(4)
    where = [place(own, four, core) for core in (c, 1 - c) for own in (y, zh)]
    where = jnp.concatenate(where + [c[None]]).astype(jnp.int32)

    tokens = nx * middle
    shape = (tokens, hidden_width)
    flops = 2 * tokens * width * hidden_width
    halves = [((4, 4, width // 32, hidden_width), BF16)] * 2
    rows_of = ((tokens, width), BF16)
    normed_all, hidden, slope = computed(
        pre_kernel, flops, [rows_of, (shape, BF16), (shape, F32)], *normed_pieces, up_weight
    )
    grad_all, *down = computed(down_kernel, flops, [rows_of] + halves, where, *grad_pieces, hidden)
    pre_grad, *up = computed(
        up_kernel, 2 * flops, [(shape, BF16)] + halves, where, grad_all, normed_all, slope, down_weight
    )

    blocks = pre_grad.reshape(nx, middle, hidden_width)
    first, second = jnp.where(x % 2 == 0, 2, 1), jnp.where(x % 2 == 0, 1, 2)
    blocks = jnp.stack([blocks[0], pick(blocks, second, 0), pick(blocks, first, 0), blocks[3]])

    fence = lax.optimization_barrier

    def to_core(term):
        return lax.ppermute(term[1], "c", [(0, 1), (1, 0)])

    def to_y(term, core):
        return paired(added(term[0][2:], core[2:]).astype(BF16), "y", 0)

    def to_second_y(term, core, got):
        return paired(added(term[0][1], core[1], got[1]).astype(BF16), "y", 1)

    def summed(term, at):
        keep, core, got, second = term
        return added(keep[0, at], core[0, at], got[0, at], second[at])

    def to_z(*term):
        return paired(summed(term, slice(2, 4)).astype(BF16), "zh", 0)

    def to_second_z(term, got):
        return paired(added(summed(term, 1), got[1]).astype(BF16), "zh", 1)

    down_core, up_core = to_core(down), to_core(up)
    down_y, up_y = to_y(down, down_core), to_y(up, up_core)
    up_core, blocks = fence((up_core, blocks))
    full_term = jnp.einsum("xtf,df->xtd", blocks, up_weight, preferred_element_type=F32)
    full_term = full_term.astype(BF16)
    x_first = paired(full_term[2:], "x", 0)

    down_y2 = to_second_y(down, down_core, down_y)
    down_z = to_z(down[0], down_core, down_y, down_y2)
    down_y2, x_first = fence((down_y2, x_first))
    x_second = paired(added(full_term[1], x_first[1]).astype(BF16), "x", 1)
    up_y, x_second = fence((up_y, x_second))
    up_y2 = to_second_y(up, up_core, up_y)
    up_z = to_z(up[0], up_core, up_y, up_y2)
    own = added(full_term[0], x_first[0], x_second)

    def halved(own, distance):
        half = own.shape[0] // 2
        return added(own[:half], swap(own[half:].astype(BF16), distance))

    up_y2, own = fence((up_y2, own))
    own = halved(own, 1)
    down, up = (down[0], down_core, down_y, down_y2), (up[0], up_core, up_y, up_y2)
    down_z, own = fence((down_z, own))
    down_z2, up_z2 = to_second_z(down, down_z), to_second_z(up, up_z)
    own = halved(own, 2)
    up_z, own = fence((up_z, own))
    normed_grad = halved(own, 4)
    down_grad = added(summed(down, 0), down_z[0], down_z2).T
    up_grad = added(summed(up, 0), up_z[0], up_z2)

    rstd = stats[:, 1:2]
    xhat = (layer_input.astype(F32) - stats[:, 0:1]) * rstd
    g = normed_grad * norm_gain_vector
    back = rstd * (
        g
        - jnp.mean(g, axis=1, keepdims=True)
        - xhat * jnp.mean(g * xhat, axis=1, keepdims=True)
    )
    input_grad = (out_grad.astype(F32) + back).astype(BF16)
    return (input_grad, up_grad, down_grad)


def solution(mesh):
    fine = Mesh(mesh.devices.reshape(SIZES), NAMES)
    dp, mp, both = ("zh", "y", "c"), ("x", "zl"), NAMES
    return jax.shard_map(
        shards,
        mesh=fine,
        in_specs=(P(both, None), P(both, None), P(), P(None, mp), P(mp, None)),
        out_specs=(P(both, None), P(dp, mp), P(mp, dp)),
        check_vma=False,
    )
```

```python
import math

import jax
import jax.numpy as jnp
from jax import lax
from jax.experimental import pallas as pl
from jax.experimental.pallas import tpu as pltpu
from jax.sharding import Mesh
from jax.sharding import PartitionSpec as P

BF16, F32 = jnp.bfloat16, jnp.float32
NAMES = ("zh", "y", "c", "x", "zl")
SIZES = (4, 4, 2, 4, 8)


def gelu_parts(v):
    cdf = 0.5 * (1.0 + jax.scipy.special.erf(v / math.sqrt(2.0)))
    return v * cdf, cdf + v * jnp.exp(-0.5 * v * v) / math.sqrt(2.0 * math.pi)


def swap(block, distance):
    return lax.ppermute(block, "zl", [(i, i ^ distance) for i in range(8)])


def x_moves(way):
    moves = [(4 * c + i, 4 * c + (i + way * (1 - 2 * c)) % 4) for c in range(2) for i in range(4)]
    return lambda block: lax.ppermute(block, ("c", "x"), moves)


def pairs(axis, step):
    flip = {(c, s): 1 if c == s else 3 for c in range(2) for s in range(2)}
    if axis == "x":
        return ("c", "x"), [
            (4 * c + i, 4 * c + (i ^ flip[c, step])) for c in range(2) for i in range(4)
        ]
    return (axis, "c"), [
        (2 * i + c, 2 * (i ^ flip[c, step]) + c) for c in range(2) for i in range(4)
    ]


def paired(block, axis, step):
    names, moves = pairs(axis, step)
    return lax.ppermute(block, names, moves)


def place(own, other, c):
    apart = own ^ other
    odd = jnp.where(c == 0, (5 - apart) // 2, (apart + 1) // 2)
    return jnp.where(apart == 0, 0, jnp.where(apart == 2, 3, odd))


def added(*terms):
    total = terms[0].astype(F32)
    for term in terms[1:]:
        total = total + term.astype(F32)
    return total


def pick(array, index, axis):
    return lax.dynamic_index_in_dim(array, index, axis, keepdims=False)


def pack_kernel(layer_input, out_grad, gain, packed, stats, rows_in, grad_in, gain_in, sems):
    loads = [
        pltpu.make_async_copy(source, target, sems.at[k])
        for k, (source, target) in enumerate(
            ((layer_input, rows_in), (gain, gain_in), (out_grad, grad_in))
        )
    ]
    for load in loads:
        load.start()
    rows, width = rows_in.shape
    half = width // 2
    loads[0].wait()
    xf = rows_in[...].astype(F32)
    mean = jnp.mean(xf, axis=1, keepdims=True)
    centered = xf - mean
    rstd = 1.0 / jnp.sqrt(jnp.mean(centered * centered, axis=1, keepdims=True) + 1e-06)
    loads[1].wait()
    normed = (centered * rstd * gain_in[...]).astype(BF16)
    loads[2].wait()
    for at, block in enumerate((normed, grad_in[...])):
        packed[2 * at * rows : (2 * at + 1) * rows] = block[:, :half]
        packed[(2 * at + 1) * rows : (2 * at + 2) * rows] = block[:, half:]
    stats[:, 0:1] = mean
    stats[:, 1:2] = rstd


def pack(layer_input, out_grad, gain):
    rows, width = layer_input.shape
    vmem = pl.BlockSpec(memory_space=pltpu.VMEM)
    return pl.pallas_call(
        pack_kernel,
        out_shape=(
            jax.ShapeDtypeStruct((4 * rows, width // 2), BF16),
            jax.ShapeDtypeStruct((rows, 2), F32),
        ),
        in_specs=[pl.BlockSpec(memory_space=pl.ANY)] * 3,
        out_specs=(vmem, vmem),
        scratch_shapes=[
            pltpu.VMEM((rows, width), BF16),
            pltpu.VMEM((rows, width), BF16),
            pltpu.VMEM((1, width), F32),
            pltpu.SemaphoreType.DMA((3,)),
        ],
        compiler_params=pltpu.CompilerParams(vmem_limit_bytes=4 * 1024 * 1024),
    )(layer_input, out_grad, gain[None])


def unpack_kernel(own, far, block):
    rows, half = own.shape[0] // 4, own.shape[1]
    for at in range(2):
        for k, source in enumerate((own, far)):
            to = slice((2 * at + k) * rows, (2 * at + k + 1) * rows)
            block[to, :half] = source[2 * at * rows : (2 * at + 1) * rows]
            block[to, half:] = source[(2 * at + 1) * rows : (2 * at + 2) * rows]


def join_kernel(*refs):
    pieces, outs = refs[:4], refs[4:]
    rows = pieces[0].shape[0] // 2
    for k, piece in enumerate(pieces):
        for at, out in enumerate(outs):
            out[k * rows : (k + 1) * rows] = piece[at * rows : (at + 1) * rows]


def in_vmem(kernel, outs, *operands):
    return pl.pallas_call(
        kernel,
        out_shape=[jax.ShapeDtypeStruct(*out) for out in outs],
        in_specs=[pl.BlockSpec(memory_space=pltpu.VMEM)] * len(operands),
        out_specs=[pl.BlockSpec(memory_space=pltpu.VMEM)] * len(outs),
        compiler_params=pltpu.CompilerParams(vmem_limit_bytes=8 * 1024 * 1024),
    )(*operands)


def pre_kernel(*refs):
    pieces, (weight, rows, hidden, slope) = refs[:4], refs[4:]
    count = pieces[0].shape[0]
    for k, piece in enumerate(pieces):
        rows[k * count : (k + 1) * count] = piece[...]
    pre = jnp.dot(rows[...], weight[...], preferred_element_type=F32)
    value, slope[...] = gelu_parts(pre)
    hidden[...] = value.astype(BF16)


def write_halves(where, left, right, keep, send):
    part = keep.shape[2]
    c = where[16]
    for g in range(8):
        columns = slice(4 * part * g, 4 * part * (g + 1))
        term = lax.dot_general(
            left[:, columns], right, (((0,), (0,)), ((), ())), preferred_element_type=F32
        ).astype(BF16)
        for pair in range(2):
            at_y, there_y = (where[at + 2 * (g % 2) + pair] for at in (0, 8))
            at_z, there_z = (where[at + g // 2] for at in (4, 12))
            low = term[2 * pair * part : (2 * pair + 1) * part]
            high = term[(2 * pair + 1) * part : (2 * pair + 2) * part]
            keep[at_y, at_z] = jnp.where(c == 0, low, high)
            send[there_y, there_z] = jnp.where(c == 0, high, low)


def down_kernel(where, *refs):
    pieces, (hidden, rows, keep, send) = refs[:4], refs[4:]
    count = pieces[0].shape[0]
    for k, piece in enumerate(pieces):
        rows[k * count : (k + 1) * count] = piece[...]
    write_halves(where, rows, hidden[...], keep, send)


def up_kernel(where, grad, normed, slope, weight, pre_grad, keep, send):
    hidden_grad = lax.dot_general(
        grad[...], weight[...], (((1,), (1,)), ((), ())), preferred_element_type=F32
    )
    product = (hidden_grad * slope[...]).astype(BF16)
    pre_grad[...] = product
    write_halves(where, normed, product, keep, send)


def computed(kernel, flops, outs, *operands):
    vmem = pl.BlockSpec(memory_space=pltpu.VMEM)
    scalars = [operand.dtype == jnp.int32 for operand in operands]
    return pl.pallas_call(
        kernel,
        out_shape=[jax.ShapeDtypeStruct(*out) for out in outs],
        in_specs=[pl.BlockSpec(memory_space=pltpu.SMEM) if scalar else vmem for scalar in scalars],
        out_specs=[vmem] * len(outs),
        compiler_params=pltpu.CompilerParams(vmem_limit_bytes=12 * 1024 * 1024),
        cost_estimate=pl.CostEstimate(
            flops=flops, bytes_accessed=8 * 1024 * 1024, transcendentals=0
        ),
    )(*operands)


def shards(layer_input, out_grad, norm_gain_vector, up_weight, down_weight):
    nx, nzl = SIZES[3:]
    rows, width = layer_input.shape
    hidden_width = up_weight.shape[1]
    zh, y, c = lax.axis_index("zh"), lax.axis_index("y"), lax.axis_index("c")
    x, zl = lax.axis_index("x"), lax.axis_index("zl")

    packed, stats = pack(layer_input, out_grad, norm_gain_vector)
    (block,) = in_vmem(unpack_kernel, [((4 * rows, width), BF16)], packed, swap(packed, 4))
    middle = nzl * rows
    normed, grad = in_vmem(
        join_kernel, [((middle, width), BF16)] * 2, block, *[swap(block, k) for k in (2, 1, 3)]
    )
    ahead, back = x_moves(1), x_moves(-1)
    normed_ahead, grad_ahead = ahead(normed), ahead(grad)
    normed_pieces = normed, normed_ahead, back(normed), ahead(normed_ahead)
    grad_pieces = grad, grad_ahead, back(grad), ahead(grad_ahead)

    four = jnp.arange(4)
    where = [place(own, four, core) for core in (c, 1 - c) for own in (y, zh)]
    where = jnp.concatenate(where + [c[None]]).astype(jnp.int32)

    tokens = nx * middle
    shape = (tokens, hidden_width)
    flops = 2 * tokens * width * hidden_width
    halves = [((4, 4, width // 32, hidden_width), BF16)] * 2
    rows_of = ((tokens, width), BF16)
    normed_all, hidden, slope = computed(
        pre_kernel, flops, [rows_of, (shape, BF16), (shape, F32)], *normed_pieces, up_weight
    )
    grad_all, *down = computed(down_kernel, flops, [rows_of] + halves, where, *grad_pieces, hidden)
    pre_grad, *up = computed(
        up_kernel, 2 * flops, [(shape, BF16)] + halves, where, grad_all, normed_all, slope, down_weight
    )

    blocks = pre_grad.reshape(nx, middle, hidden_width)
    first, second = jnp.where(x % 2 == 0, 2, 1), jnp.where(x % 2 == 0, 1, 2)
    blocks = jnp.stack([blocks[0], pick(blocks, second, 0), pick(blocks, first, 0), blocks[3]])

    fence = lax.optimization_barrier

    def to_core(term):
        return lax.ppermute(term[1], "c", [(0, 1), (1, 0)])

    def to_y(term, core):
        return paired(added(term[0][2:], core[2:]).astype(BF16), "y", 0)

    def to_second_y(term, core, got):
        return paired(added(term[0][1], core[1], got[1]).astype(BF16), "y", 1)

    def summed(term, at):
        keep, core, got, second = term
        return added(keep[0, at], core[0, at], got[0, at], second[at])

    def to_z(*term):
        return paired(summed(term, slice(2, 4)).astype(BF16), "zh", 0)

    def to_second_z(term, got):
        return paired(added(summed(term, 1), got[1]).astype(BF16), "zh", 1)

    down_core, up_core = to_core(down), to_core(up)
    up_core_now, blocks = fence((up_core, blocks))
    full_term = jnp.einsum("xtf,df->xtd", blocks, up_weight, preferred_element_type=F32)
    full_term = full_term.astype(BF16)
    x_first = paired(full_term[2:], "x", 0)
    down_y, up_y = to_y(down, down_core), to_y(up, up_core)
    up_core = up_core_now
    down_y2 = to_second_y(down, down_core, down_y)
    down_z = to_z(down[0], down_core, down_y, down_y2)
    down_y2, x_first, up_y = fence((down_y2, x_first, up_y))
    up_y2 = to_second_y(up, up_core, up_y)
    up_z = to_z(up[0], up_core, up_y, up_y2)
    x_second = paired(added(full_term[1], x_first[1]).astype(BF16), "x", 1)
    own = added(full_term[0], x_first[0], x_second)

    def halved(own, distance):
        half = own.shape[0] // 2
        return added(own[:half], swap(own[half:].astype(BF16), distance))

    up_y2, own = fence((up_y2, own))
    own = halved(own, 1)
    down, up = (down[0], down_core, down_y, down_y2), (up[0], up_core, up_y, up_y2)
    down_z, own = fence((down_z, own))
    down_z2, up_z2 = to_second_z(down, down_z), to_second_z(up, up_z)
    own = halved(own, 2)
    up_z, own = fence((up_z, own))
    normed_grad = halved(own, 4)
    down_grad = added(summed(down, 0), down_z[0], down_z2).T
    up_grad = added(summed(up, 0), up_z[0], up_z2)

    rstd = stats[:, 1:2]
    xhat = (layer_input.astype(F32) - stats[:, 0:1]) * rstd
    g = normed_grad * norm_gain_vector
    back = rstd * (
        g
        - jnp.mean(g, axis=1, keepdims=True)
        - xhat * jnp.mean(g * xhat, axis=1, keepdims=True)
    )
    input_grad = (out_grad.astype(F32) + back).astype(BF16)
    return (input_grad, up_grad, down_grad)


def solution(mesh):
    fine = Mesh(mesh.devices.reshape(SIZES), NAMES)
    dp, mp, both = ("zh", "y", "c"), ("x", "zl"), NAMES
    return jax.shard_map(
        shards,
        mesh=fine,
        in_specs=(P(both, None), P(both, None), P(), P(None, mp), P(mp, None)),
        out_specs=(P(both, None), P(dp, mp), P(mp, dp)),
        check_vma=False,
    )
```

```python
import math

import jax
import jax.numpy as jnp
from jax import lax
from jax.experimental import pallas as pl
from jax.experimental.pallas import tpu as pltpu
from jax.sharding import Mesh
from jax.sharding import PartitionSpec as P

BF16, F32 = jnp.bfloat16, jnp.float32
NAMES = ("zh", "y", "c", "x", "zl")
SIZES = (4, 4, 2, 4, 8)


def gelu_parts(v):
    cdf = 0.5 * (1.0 + jax.scipy.special.erf(v / math.sqrt(2.0)))
    return v * cdf, cdf + v * jnp.exp(-0.5 * v * v) / math.sqrt(2.0 * math.pi)


def swap(block, distance):
    return lax.ppermute(block, "zl", [(i, i ^ distance) for i in range(8)])


def x_moves(way):
    moves = [(4 * c + i, 4 * c + (i + way * (1 - 2 * c)) % 4) for c in range(2) for i in range(4)]
    return lambda block: lax.ppermute(block, ("c", "x"), moves)


def pairs(axis, step):
    flip = {(c, s): 1 if c == s else 3 for c in range(2) for s in range(2)}
    if axis == "x":
        return ("c", "x"), [
            (4 * c + i, 4 * c + (i ^ flip[c, step])) for c in range(2) for i in range(4)
        ]
    return (axis, "c"), [
        (2 * i + c, 2 * (i ^ flip[c, step]) + c) for c in range(2) for i in range(4)
    ]


def paired(block, axis, step):
    names, moves = pairs(axis, step)
    return lax.ppermute(block, names, moves)


def place(own, other, c):
    apart = own ^ other
    odd = jnp.where(c == 0, (5 - apart) // 2, (apart + 1) // 2)
    return jnp.where(apart == 0, 0, jnp.where(apart == 2, 3, odd))


def added(*terms):
    total = terms[0].astype(F32)
    for term in terms[1:]:
        total = total + term.astype(F32)
    return total


def pick(array, index, axis):
    return lax.dynamic_index_in_dim(array, index, axis, keepdims=False)


def pack_kernel(layer_input, out_grad, gain, packed, stats, rows_in, grad_in, gain_in, sems):
    loads = [
        pltpu.make_async_copy(source, target, sems.at[k])
        for k, (source, target) in enumerate(
            ((layer_input, rows_in), (gain, gain_in), (out_grad, grad_in))
        )
    ]
    for load in loads:
        load.start()
    rows, width = rows_in.shape
    half = width // 2
    loads[0].wait()
    xf = rows_in[...].astype(F32)
    mean = jnp.mean(xf, axis=1, keepdims=True)
    centered = xf - mean
    rstd = 1.0 / jnp.sqrt(jnp.mean(centered * centered, axis=1, keepdims=True) + 1e-06)
    loads[1].wait()
    normed = (centered * rstd * gain_in[...]).astype(BF16)
    loads[2].wait()
    for at, block in enumerate((normed, grad_in[...])):
        packed[2 * at * rows : (2 * at + 1) * rows] = block[:, :half]
        packed[(2 * at + 1) * rows : (2 * at + 2) * rows] = block[:, half:]
    stats[:, 0:1] = mean
    stats[:, 1:2] = rstd


def pack(layer_input, out_grad, gain):
    rows, width = layer_input.shape
    vmem = pl.BlockSpec(memory_space=pltpu.VMEM)
    return pl.pallas_call(
        pack_kernel,
        out_shape=(
            jax.ShapeDtypeStruct((4 * rows, width // 2), BF16),
            jax.ShapeDtypeStruct((rows, 2), F32),
        ),
        in_specs=[pl.BlockSpec(memory_space=pl.ANY)] * 3,
        out_specs=(vmem, vmem),
        scratch_shapes=[
            pltpu.VMEM((rows, width), BF16),
            pltpu.VMEM((rows, width), BF16),
            pltpu.VMEM((1, width), F32),
            pltpu.SemaphoreType.DMA((3,)),
        ],
        compiler_params=pltpu.CompilerParams(vmem_limit_bytes=4 * 1024 * 1024),
    )(layer_input, out_grad, gain[None])


def unpack_kernel(own, far, block):
    rows, half = own.shape[0] // 4, own.shape[1]
    for at in range(2):
        for k, source in enumerate((own, far)):
            to = slice((2 * at + k) * rows, (2 * at + k + 1) * rows)
            block[to, :half] = source[2 * at * rows : (2 * at + 1) * rows]
            block[to, half:] = source[(2 * at + 1) * rows : (2 * at + 2) * rows]


def join_kernel(*refs):
    pieces, outs = refs[:4], refs[4:]
    rows = pieces[0].shape[0] // 2
    for k, piece in enumerate(pieces):
        for at, out in enumerate(outs):
            out[k * rows : (k + 1) * rows] = piece[at * rows : (at + 1) * rows]


def in_vmem(kernel, outs, *operands):
    return pl.pallas_call(
        kernel,
        out_shape=[jax.ShapeDtypeStruct(*out) for out in outs],
        in_specs=[pl.BlockSpec(memory_space=pltpu.VMEM)] * len(operands),
        out_specs=[pl.BlockSpec(memory_space=pltpu.VMEM)] * len(outs),
        compiler_params=pltpu.CompilerParams(vmem_limit_bytes=8 * 1024 * 1024),
    )(*operands)


def pre_kernel(*refs):
    pieces, (weight, rows, hidden, slope) = refs[:4], refs[4:]
    count = pieces[0].shape[0]
    for k, piece in enumerate(pieces):
        rows[k * count : (k + 1) * count] = piece[...]
    pre = jnp.dot(rows[...], weight[...], preferred_element_type=F32)
    value, slope[...] = gelu_parts(pre)
    hidden[...] = value.astype(BF16)


def write_halves(where, left, right, keep, send):
    part = keep.shape[2]
    c = where[16]
    for g in range(8):
        columns = slice(4 * part * g, 4 * part * (g + 1))
        term = lax.dot_general(
            left[:, columns], right, (((0,), (0,)), ((), ())), preferred_element_type=F32
        ).astype(BF16)
        for pair in range(2):
            at_y, there_y = (where[at + 2 * (g % 2) + pair] for at in (0, 8))
            at_z, there_z = (where[at + g // 2] for at in (4, 12))
            low = term[2 * pair * part : (2 * pair + 1) * part]
            high = term[(2 * pair + 1) * part : (2 * pair + 2) * part]
            keep[at_y, at_z] = jnp.where(c == 0, low, high)
            send[there_y, there_z] = jnp.where(c == 0, high, low)


def down_kernel(where, *refs):
    pieces, (hidden, rows, keep, send) = refs[:4], refs[4:]
    count = pieces[0].shape[0]
    for k, piece in enumerate(pieces):
        rows[k * count : (k + 1) * count] = piece[...]
    write_halves(where, rows, hidden[...], keep, send)


def up_kernel(where, grad, normed, slope, weight, pre_grad, keep, send):
    hidden_grad = lax.dot_general(
        grad[...], weight[...], (((1,), (1,)), ((), ())), preferred_element_type=F32
    )
    product = (hidden_grad * slope[...]).astype(BF16)
    pre_grad[...] = product
    write_halves(where, normed, product, keep, send)


def computed(kernel, flops, outs, *operands):
    vmem = pl.BlockSpec(memory_space=pltpu.VMEM)
    scalars = [operand.dtype == jnp.int32 for operand in operands]
    return pl.pallas_call(
        kernel,
        out_shape=[jax.ShapeDtypeStruct(*out) for out in outs],
        in_specs=[pl.BlockSpec(memory_space=pltpu.SMEM) if scalar else vmem for scalar in scalars],
        out_specs=[vmem] * len(outs),
        compiler_params=pltpu.CompilerParams(vmem_limit_bytes=12 * 1024 * 1024),
        cost_estimate=pl.CostEstimate(
            flops=flops, bytes_accessed=8 * 1024 * 1024, transcendentals=0
        ),
    )(*operands)


def shards(layer_input, out_grad, norm_gain_vector, up_weight, down_weight):
    nx, nzl = SIZES[3:]
    rows, width = layer_input.shape
    hidden_width = up_weight.shape[1]
    zh, y, c = lax.axis_index("zh"), lax.axis_index("y"), lax.axis_index("c")
    x, zl = lax.axis_index("x"), lax.axis_index("zl")

    packed, stats = pack(layer_input, out_grad, norm_gain_vector)
    (block,) = in_vmem(unpack_kernel, [((4 * rows, width), BF16)], packed, swap(packed, 4))
    middle = nzl * rows
    normed, grad = in_vmem(
        join_kernel, [((middle, width), BF16)] * 2, block, *[swap(block, k) for k in (2, 1, 3)]
    )
    ahead, back = x_moves(1), x_moves(-1)
    normed_ahead, grad_ahead = ahead(normed), ahead(grad)
    normed_pieces = normed, normed_ahead, back(normed), ahead(normed_ahead)
    grad_pieces = grad, grad_ahead, back(grad), ahead(grad_ahead)

    four = jnp.arange(4)
    where = [place(own, four, core) for core in (c, 1 - c) for own in (y, zh)]
    where = jnp.concatenate(where + [c[None]]).astype(jnp.int32)

    tokens = nx * middle
    shape = (tokens, hidden_width)
    flops = 2 * tokens * width * hidden_width
    halves = [((4, 4, width // 32, hidden_width), BF16)] * 2
    rows_of = ((tokens, width), BF16)
    normed_all, hidden, slope = computed(
        pre_kernel, flops, [rows_of, (shape, BF16), (shape, F32)], *normed_pieces, up_weight
    )
    grad_all, *down = computed(down_kernel, flops, [rows_of] + halves, where, *grad_pieces, hidden)
    pre_grad, *up = computed(
        up_kernel, 2 * flops, [(shape, BF16)] + halves, where, grad_all, normed_all, slope, down_weight
    )

    blocks = pre_grad.reshape(nx, middle, hidden_width)
    first, second = jnp.where(x % 2 == 0, 2, 1), jnp.where(x % 2 == 0, 1, 2)
    blocks = jnp.stack([blocks[0], pick(blocks, second, 0), pick(blocks, first, 0), blocks[3]])

    fence = lax.optimization_barrier

    def to_core(term):
        return lax.ppermute(term[1], "c", [(0, 1), (1, 0)])

    def to_y(term, core):
        return paired(added(term[0][2:], core[2:]).astype(BF16), "y", 0)

    def to_second_y(term, core, got):
        return paired(added(term[0][1], core[1], got[1]).astype(BF16), "y", 1)

    def summed(term, at):
        keep, core, got, second = term
        return added(keep[0, at], core[0, at], got[0, at], second[at])

    def to_z(*term):
        return paired(summed(term, slice(2, 4)).astype(BF16), "zh", 0)

    def to_second_z(term, got):
        return paired(added(summed(term, 1), got[1]).astype(BF16), "zh", 1)

    down_core, up_core = to_core(down), to_core(up)
    up_core_now, blocks = fence((up_core, blocks))
    full_term = jnp.einsum("xtf,df->xtd", blocks, up_weight, preferred_element_type=F32)
    full_term = full_term.astype(BF16)
    x_first = paired(full_term[2:], "x", 0)
    down_y, up_y = to_y(down, down_core), to_y(up, up_core)
    up_core = up_core_now
    down_y2 = to_second_y(down, down_core, down_y)
    down_z = to_z(down[0], down_core, down_y, down_y2)
    down_y2, x_first, up_y = fence((down_y2, x_first, up_y))
    up_y2 = to_second_y(up, up_core, up_y)
    up_z = to_z(up[0], up_core, up_y, up_y2)
    x_second = paired(added(full_term[1], x_first[1]).astype(BF16), "x", 1)
    own = added(full_term[0], x_first[0], x_second)

    def halved(own, distance):
        half = own.shape[0] // 2
        return added(own[:half], swap(own[half:].astype(BF16), distance))

    own = halved(own, 1)
    down, up = (down[0], down_core, down_y, down_y2), (up[0], up_core, up_y, up_y2)
    down_z, own = fence((down_z, own))
    down_z2, up_z2 = to_second_z(down, down_z), to_second_z(up, up_z)
    own = halved(own, 2)
    up_z, own = fence((up_z, own))
    normed_grad = halved(own, 4)
    down_grad = added(summed(down, 0), down_z[0], down_z2).T
    up_grad = added(summed(up, 0), up_z[0], up_z2)

    rstd = stats[:, 1:2]
    xhat = (layer_input.astype(F32) - stats[:, 0:1]) * rstd
    g = normed_grad * norm_gain_vector
    back = rstd * (
        g
        - jnp.mean(g, axis=1, keepdims=True)
        - xhat * jnp.mean(g * xhat, axis=1, keepdims=True)
    )
    input_grad = (out_grad.astype(F32) + back).astype(BF16)
    return (input_grad, up_grad, down_grad)


def solution(mesh):
    fine = Mesh(mesh.devices.reshape(SIZES), NAMES)
    dp, mp, both = ("zh", "y", "c"), ("x", "zl"), NAMES
    return jax.shard_map(
        shards,
        mesh=fine,
        in_specs=(P(both, None), P(both, None), P(), P(None, mp), P(mp, None)),
        out_specs=(P(both, None), P(dp, mp), P(mp, dp)),
        check_vma=False,
    )
```

```python
import math

import jax
import jax.numpy as jnp
from jax import lax
from jax.experimental import pallas as pl
from jax.experimental.pallas import tpu as pltpu
from jax.sharding import Mesh
from jax.sharding import PartitionSpec as P

BF16, F32 = jnp.bfloat16, jnp.float32
NAMES = ("zh", "y", "c", "x", "zl")
SIZES = (4, 4, 2, 4, 8)


def gelu_parts(v):
    cdf = 0.5 * (1.0 + jax.scipy.special.erf(v / math.sqrt(2.0)))
    return v * cdf, cdf + v * jnp.exp(-0.5 * v * v) / math.sqrt(2.0 * math.pi)


def swap(block, distance):
    return lax.ppermute(block, "zl", [(i, i ^ distance) for i in range(8)])


def x_moves(way):
    moves = [(4 * c + i, 4 * c + (i + way * (1 - 2 * c)) % 4) for c in range(2) for i in range(4)]
    return lambda block: lax.ppermute(block, ("c", "x"), moves)


def pairs(axis, step):
    flip = {(c, s): 1 if c == s else 3 for c in range(2) for s in range(2)}
    if axis == "x":
        return ("c", "x"), [
            (4 * c + i, 4 * c + (i ^ flip[c, step])) for c in range(2) for i in range(4)
        ]
    return (axis, "c"), [
        (2 * i + c, 2 * (i ^ flip[c, step]) + c) for c in range(2) for i in range(4)
    ]


def paired(block, axis, step):
    names, moves = pairs(axis, step)
    return lax.ppermute(block, names, moves)


def place(own, other, c):
    apart = own ^ other
    odd = jnp.where(c == 0, (5 - apart) // 2, (apart + 1) // 2)
    return jnp.where(apart == 0, 0, jnp.where(apart == 2, 3, odd))


def added(*terms):
    total = terms[0].astype(F32)
    for term in terms[1:]:
        total = total + term.astype(F32)
    return total


def pick(array, index, axis):
    return lax.dynamic_index_in_dim(array, index, axis, keepdims=False)


def pack_kernel(layer_input, out_grad, gain, packed, stats, rows_in, grad_in, gain_in, sems):
    loads = [
        pltpu.make_async_copy(source, target, sems.at[k])
        for k, (source, target) in enumerate(
            ((layer_input, rows_in), (gain, gain_in), (out_grad, grad_in))
        )
    ]
    for load in loads:
        load.start()
    rows, width = rows_in.shape
    half = width // 2
    loads[0].wait()
    xf = rows_in[...].astype(F32)
    mean = jnp.mean(xf, axis=1, keepdims=True)
    centered = xf - mean
    rstd = 1.0 / jnp.sqrt(jnp.mean(centered * centered, axis=1, keepdims=True) + 1e-06)
    loads[1].wait()
    normed = (centered * rstd * gain_in[...]).astype(BF16)
    loads[2].wait()
    for at, block in enumerate((normed, grad_in[...])):
        packed[2 * at * rows : (2 * at + 1) * rows] = block[:, :half]
        packed[(2 * at + 1) * rows : (2 * at + 2) * rows] = block[:, half:]
    stats[:, 0:1] = mean
    stats[:, 1:2] = rstd


def pack(layer_input, out_grad, gain):
    rows, width = layer_input.shape
    vmem = pl.BlockSpec(memory_space=pltpu.VMEM)
    return pl.pallas_call(
        pack_kernel,
        out_shape=(
            jax.ShapeDtypeStruct((4 * rows, width // 2), BF16),
            jax.ShapeDtypeStruct((rows, 2), F32),
        ),
        in_specs=[pl.BlockSpec(memory_space=pl.ANY)] * 3,
        out_specs=(vmem, vmem),
        scratch_shapes=[
            pltpu.VMEM((rows, width), BF16),
            pltpu.VMEM((rows, width), BF16),
            pltpu.VMEM((1, width), F32),
            pltpu.SemaphoreType.DMA((3,)),
        ],
        compiler_params=pltpu.CompilerParams(vmem_limit_bytes=4 * 1024 * 1024),
    )(layer_input, out_grad, gain[None])


def unpack_kernel(own, far, block):
    rows, half = own.shape[0] // 4, own.shape[1]
    for at in range(2):
        for k, source in enumerate((own, far)):
            to = slice((2 * at + k) * rows, (2 * at + k + 1) * rows)
            block[to, :half] = source[2 * at * rows : (2 * at + 1) * rows]
            block[to, half:] = source[(2 * at + 1) * rows : (2 * at + 2) * rows]


def join_kernel(*refs):
    pieces, outs = refs[:4], refs[4:]
    rows = pieces[0].shape[0] // 2
    for k, piece in enumerate(pieces):
        for at, out in enumerate(outs):
            out[k * rows : (k + 1) * rows] = piece[at * rows : (at + 1) * rows]


def in_vmem(kernel, outs, *operands):
    return pl.pallas_call(
        kernel,
        out_shape=[jax.ShapeDtypeStruct(*out) for out in outs],
        in_specs=[pl.BlockSpec(memory_space=pltpu.VMEM)] * len(operands),
        out_specs=[pl.BlockSpec(memory_space=pltpu.VMEM)] * len(outs),
        compiler_params=pltpu.CompilerParams(vmem_limit_bytes=8 * 1024 * 1024),
    )(*operands)


def pre_kernel(*refs):
    pieces, (weight, rows, hidden, slope) = refs[:4], refs[4:]
    count = pieces[0].shape[0]
    for k, piece in enumerate(pieces):
        rows[k * count : (k + 1) * count] = piece[...]
    pre = jnp.dot(rows[...], weight[...], preferred_element_type=F32)
    value, slope[...] = gelu_parts(pre)
    hidden[...] = value.astype(BF16)


def write_halves(where, left, right, keep, send):
    part = keep.shape[2]
    c = where[16]
    for g in range(8):
        columns = slice(4 * part * g, 4 * part * (g + 1))
        term = lax.dot_general(
            left[:, columns], right, (((0,), (0,)), ((), ())), preferred_element_type=F32
        ).astype(BF16)
        for pair in range(2):
            at_y, there_y = (where[at + 2 * (g % 2) + pair] for at in (0, 8))
            at_z, there_z = (where[at + g // 2] for at in (4, 12))
            low = term[2 * pair * part : (2 * pair + 1) * part]
            high = term[(2 * pair + 1) * part : (2 * pair + 2) * part]
            keep[at_y, at_z] = jnp.where(c == 0, low, high)
            send[there_y, there_z] = jnp.where(c == 0, high, low)


def down_kernel(where, *refs):
    pieces, (hidden, rows, keep, send) = refs[:4], refs[4:]
    count = pieces[0].shape[0]
    for k, piece in enumerate(pieces):
        rows[k * count : (k + 1) * count] = piece[...]
    write_halves(where, rows, hidden[...], keep, send)


def up_kernel(where, grad, normed, slope, weight, pre_grad, keep, send):
    hidden_grad = lax.dot_general(
        grad[...], weight[...], (((1,), (1,)), ((), ())), preferred_element_type=F32
    )
    product = (hidden_grad * slope[...]).astype(BF16)
    pre_grad[...] = product
    write_halves(where, normed, product, keep, send)


def computed(kernel, flops, outs, *operands):
    vmem = pl.BlockSpec(memory_space=pltpu.VMEM)
    scalars = [operand.dtype == jnp.int32 for operand in operands]
    return pl.pallas_call(
        kernel,
        out_shape=[jax.ShapeDtypeStruct(*out) for out in outs],
        in_specs=[pl.BlockSpec(memory_space=pltpu.SMEM) if scalar else vmem for scalar in scalars],
        out_specs=[vmem] * len(outs),
        compiler_params=pltpu.CompilerParams(vmem_limit_bytes=12 * 1024 * 1024),
        cost_estimate=pl.CostEstimate(
            flops=flops, bytes_accessed=8 * 1024 * 1024, transcendentals=0
        ),
    )(*operands)


def shards(layer_input, out_grad, norm_gain_vector, up_weight, down_weight):
    nx, nzl = SIZES[3:]
    rows, width = layer_input.shape
    hidden_width = up_weight.shape[1]
    zh, y, c = lax.axis_index("zh"), lax.axis_index("y"), lax.axis_index("c")
    x, zl = lax.axis_index("x"), lax.axis_index("zl")

    packed, stats = pack(layer_input, out_grad, norm_gain_vector)
    (block,) = in_vmem(unpack_kernel, [((4 * rows, width), BF16)], packed, swap(packed, 4))
    middle = nzl * rows
    normed, grad = in_vmem(
        join_kernel, [((middle, width), BF16)] * 2, block, *[swap(block, k) for k in (2, 1, 3)]
    )
    ahead, back = x_moves(1), x_moves(-1)
    normed_ahead, grad_ahead = ahead(normed), ahead(grad)
    normed_pieces = normed, normed_ahead, back(normed), ahead(normed_ahead)
    grad_pieces = grad, grad_ahead, back(grad), ahead(grad_ahead)

    four = jnp.arange(4)
    where = [place(own, four, core) for core in (c, 1 - c) for own in (y, zh)]
    where = jnp.concatenate(where + [c[None]]).astype(jnp.int32)

    tokens = nx * middle
    shape = (tokens, hidden_width)
    flops = 2 * tokens * width * hidden_width
    halves = [((4, 4, width // 32, hidden_width), BF16)] * 2
    rows_of = ((tokens, width), BF16)
    normed_all, hidden, slope = computed(
        pre_kernel, flops, [rows_of, (shape, BF16), (shape, F32)], *normed_pieces, up_weight
    )
    grad_all, *down = computed(down_kernel, flops, [rows_of] + halves, where, *grad_pieces, hidden)
    pre_grad, *up = computed(
        up_kernel, 2 * flops, [(shape, BF16)] + halves, where, grad_all, normed_all, slope, down_weight
    )

    blocks = pre_grad.reshape(nx, middle, hidden_width)
    first, second = jnp.where(x % 2 == 0, 2, 1), jnp.where(x % 2 == 0, 1, 2)
    blocks = jnp.stack([blocks[0], pick(blocks, second, 0), pick(blocks, first, 0), blocks[3]])

    fence = lax.optimization_barrier

    def to_core(term):
        return lax.ppermute(term[1], "c", [(0, 1), (1, 0)])

    def to_y(term, core):
        return paired(added(term[0][2:], core[2:]).astype(BF16), "y", 0)

    def to_second_y(term, core, got):
        return paired(added(term[0][1], core[1], got[1]).astype(BF16), "y", 1)

    def summed(term, at):
        keep, core, got, second = term
        return added(keep[0, at], core[0, at], got[0, at], second[at])

    def to_z(*term):
        return paired(summed(term, slice(2, 4)).astype(BF16), "zh", 0)

    def to_second_z(term, got):
        return paired(added(summed(term, 1), got[1]).astype(BF16), "zh", 1)

    down_core, up_core = to_core(down), to_core(up)
    up_core_now, blocks = fence((up_core, blocks))
    full_term = jnp.einsum("xtf,df->xtd", blocks, up_weight, preferred_element_type=F32)
    full_term = full_term.astype(BF16)
    x_first = paired(full_term[2:], "x", 0)
    down_y, up_y = to_y(down, down_core), to_y(up, up_core)
    up_core = up_core_now
    down_y2 = to_second_y(down, down_core, down_y)
    down_z = to_z(down[0], down_core, down_y, down_y2)
    down_y2, x_first, up_y = fence((down_y2, x_first, up_y))
    up_y2 = to_second_y(up, up_core, up_y)
    up_z = to_z(up[0], up_core, up_y, up_y2)
    x_second = paired(added(full_term[1], x_first[1]).astype(BF16), "x", 1)
    own = added(full_term[0], x_first[0], x_second)

    def halved(own, distance):
        half = own.shape[0] // 2
        return added(own[:half], swap(own[half:].astype(BF16), distance))

    own = halved(own, 1)
    down, up = (down[0], down_core, down_y, down_y2), (up[0], up_core, up_y, up_y2)
    down_z, own = fence((down_z, own))
    own = halved(own, 2)
    up_z, own = fence((up_z, own))
    down_z2, up_z2 = to_second_z(down, down_z), to_second_z(up, up_z)
    normed_grad = halved(own, 4)
    down_grad = added(summed(down, 0), down_z[0], down_z2).T
    up_grad = added(summed(up, 0), up_z[0], up_z2)

    rstd = stats[:, 1:2]
    xhat = (layer_input.astype(F32) - stats[:, 0:1]) * rstd
    g = normed_grad * norm_gain_vector
    back = rstd * (
        g
        - jnp.mean(g, axis=1, keepdims=True)
        - xhat * jnp.mean(g * xhat, axis=1, keepdims=True)
    )
    input_grad = (out_grad.astype(F32) + back).astype(BF16)
    return (input_grad, up_grad, down_grad)


def solution(mesh):
    fine = Mesh(mesh.devices.reshape(SIZES), NAMES)
    dp, mp, both = ("zh", "y", "c"), ("x", "zl"), NAMES
    return jax.shard_map(
        shards,
        mesh=fine,
        in_specs=(P(both, None), P(both, None), P(), P(None, mp), P(mp, None)),
        out_specs=(P(both, None), P(dp, mp), P(mp, dp)),
        check_vma=False,
    )
```
